128 devices in a mesh: grp: 2 (over z_lo), ep: 32 (over z_hi, y, x), rep: 2 (over core).
Axes of the slice: x: 4, y: 4, z: 4 (z_hi: 2, z_lo: 2; z = z_hi * 2 + z_lo), core: 2. Of those that a mesh axis runs over, the one named last changes fastest.
Arguments:
- teacher_in: bfloat16 [128, 7168], P('ep'), may hold values from -6 to 6
- teacher_gain: float32 [7168], replicated, may hold values from 0.5 to 1.5
- routes: int32 [128, 8], P('ep'), may hold values from 0 to 31, all different within a row; in each aligned block of 4 rows (0 to 3, 4 to 7, ...) at most 2 rows name the same one
- gates: float32 [128, 8], P('ep'), may hold values from 0.1 to 0.6
- expert_gate: bfloat16 [32, 7168, 1024], P('ep', None, ('grp', 'rep')), may hold values from -0.0625 to 0.0625
- expert_up: bfloat16 [32, 7168, 1024], P('ep', None, ('grp', 'rep')), may hold values from -0.0625 to 0.0625
- expert_down: bfloat16 [32, 1024, 7168], P('ep', ('grp', 'rep')), may hold values from -0.1875 to 0.1875
- projection: bfloat16 [7168, 8192], P(None, ('grp', 'ep', 'rep')), may hold values from -0.0625 to 0.0625
- student_in: bfloat16 [128, 8192], P(None, ('grp', 'ep', 'rep')), may hold values from -6 to 6
- student_gain: float32 [8192], replicated, may hold values from 0.5 to 1.5
- student_gate: bfloat16 [8192, 14336], P(None, ('grp', 'ep', 'rep')), may hold values from -0.0625 to 0.0625
- student_up: bfloat16 [8192, 14336], P(None, ('grp', 'ep', 'rep')), may hold values from -0.0625 to 0.0625
- student_down: bfloat16 [14336, 8192], P(('grp', 'ep', 'rep')), may hold values from -0.1875 to 0.1875
Outputs:
- grad_gate: bfloat16 [8192, 14336], P(None, ('grp', 'ep', 'rep'))
- grad_up: bfloat16 [8192, 14336], P(None, ('grp', 'ep', 'rep'))
- grad_down: bfloat16 [14336, 8192], P(('grp', 'ep', 'rep'))
- mse: float32 [], replicated
The draws below stay inside these ranges and needn't reach their ends.
Inputs may be any that keep to these rules, and one draw needn't show every extreme that they name: `routes`: each token names 8 different experts. Among the 4 tokens of one index of ep, at most 2 tokens name one expert, and in every draw some expert is named by exactly 2 of them.
All inputs are finite; a program needn't handle non-finite values.
Results may differ from the reference program's by a relative error of at most 0.015.
Values may be sent and summed in bfloat16 or wider, within the bound.
No kernel may reach another device: no remote copies, remote signals or barrier semaphores. Data moves between devices by JAX's collectives and lax.ppermute only.
A program may use at most 128 MiB of HBM per device.

```python
import math
import jax
import jax.numpy as jnp
import numpy as np
from jax import lax

D_T = 7168
FE = 1024
TOP = 8
D_S = 8192
FF = 14336
TOK_EP = 4
EXPERTS = 32
CAP = 2
TOKENS = 128
N_GRP = 2
N_EP = 32
N_REP = 2


def with_spikes(result, rng, source, target, parts, factor):
    owner, partner = [(jnp.arange(result.shape[axis_at]) // (result.shape[axis_at] // parts)).reshape([-1 if axis == axis_at else 1 for axis in range(result.ndim)]) for axis_at in (source, target)]
    chosen = jax.random.permutation(rng, parts)[partner]
    strong = (owner == chosen) | (owner == (partner + parts // 2) % parts)
    return jnp.where(strong, factor * result, result)


def block_scale(stream_key, extent, shards, least, high):
    def one(axis_at, parts):
        heights = jax.random.uniform(jax.random.fold_in(jax.random.fold_in(stream_key, 6), axis_at), (parts,), jnp.float32, least / len(shards), high / len(shards))
        return jnp.repeat(jnp.exp(heights), extent[axis_at] // parts).reshape((-1,) + (1,) * (len(extent) - axis_at - 1))

    gain = one(*shards[0])
    for cut in shards[1:]:
        gain = gain * one(*cut)
    return gain


def routed_block(rng, own, number, rows, count, top, bound, lean):
    ranking = jax.random.permutation(rng, count)
    packed, ordinary = shares(count, rows * top, bound, lean, True), shares(count, rows * top, bound, lean, False)
    places = jnp.arange(count)

    def named(tallies, rotation):
        used = int((tallies > 0).sum())
        fixed = max(1, used // 4)
        moved = fixed + (places - fixed + rotation * (used - fixed)) % max(1, count - fixed)
        return jnp.zeros((count,), jnp.int32).at[ranking[jnp.where(places < fixed, places, moved)]].set(jnp.asarray(tallies, jnp.int32))

    tallies = jnp.where(number % 4 == 0, named(packed, number // 4), named(ordinary, number - number // 4 - 1))
    mixed = jax.random.permutation(jax.random.fold_in(own, 3), count)
    source_of, sink = mixed[0:count // 2 * 2:2], mixed[1:count // 2 * 2:2]
    slack = jnp.minimum(tallies[source_of] - 1, bound - tallies[sink]) // 2
    slack = jnp.where((source_of == ranking[0]) | (sink == ranking[0]) | (tallies[sink] == 0), 0, jnp.maximum(slack, 0))
    moved = jax.random.randint(jax.random.fold_in(own, 4), (count // 2,), 0, 1 << 20) % (slack + 1)
    tallies = tallies.at[source_of].add(-moved).at[sink].add(moved)
    members = jnp.searchsorted(jnp.cumsum(tallies), jnp.arange(rows * top), side="right").astype(jnp.int32)
    table = members.reshape(top, rows).T
    table = table[jax.random.permutation(jax.random.fold_in(own, 1), rows)]
    rotation = jax.random.randint(jax.random.fold_in(own, 2), (rows, 1), 0, top)
    return jnp.take_along_axis(table, (jnp.arange(top)[None, :] + rotation) % top, axis=1)


def shares(count, total, bound, skew, full):
    portions = [(1 << 20) // math.isqrt(rank ** skew) + 1 for rank in range(1, count + 1)]
    largest = bound if full else min(bound, max(-(-total // count), total * portions[0] // sum(portions)))
    least = 1 if total - largest >= count - 1 else 0
    counts, surplus = [largest] + [least] * (count - 1), total - largest - least * (count - 1)
    while surplus > 0:
        free = [i for i in range(1, count) if counts[i] < largest] or [i for i in range(1, count) if counts[i] < bound]
        whole, remaining = sum([portions[i] for i in free]), surplus
        for i in free:
            extra = min(bound - counts[i], max(1, remaining * portions[i] // whole), surplus)
            counts[i] = counts[i] + extra
            surplus = surplus - extra
    return np.array(counts)


def bell_draw(stream_key, shape, width, bound, split=(), held_as=jnp.bfloat16):
    loudness = block_scale(stream_key, shape, split, -0.22, 0.18) if split else 1.0
    array = jax.random.normal(stream_key, shape, jnp.float32) * width * loudness
    return jnp.minimum(jnp.maximum(array, -bound), bound).astype(held_as)


def noise_with(key, extent, width, limit, shards, heavy, held_as=jnp.bfloat16):
    values = width * jax.random.normal(key, extent, jnp.float32)
    if shards:
        values = values * block_scale(key, extent, shards, -0.22, 0.18)
    return jnp.clip(with_spikes(values, jax.random.fold_in(key, 3), *heavy), -limit, limit).astype(held_as)


def setup_inputs(seed: int = 0) -> dict:
    splits = jax.random.split(jax.random.key(seed), 14)
    teacher_in = bell_draw(splits[0], (TOKENS, D_T), 1.0, 6.0, ((0, 32),))
    teacher_gain = jnp.clip(1.0 + 0.1 * jax.random.normal(splits[1], (D_T,), jnp.float32), 0.5, 1.5)
    routes_keys = jax.random.split(jax.random.fold_in(splits[2], 1), TOKENS // TOK_EP)
    routes_turns = jax.random.permutation(jax.random.fold_in(splits[2], 3), TOKENS // TOK_EP)
    routes = jax.vmap(lambda own, number: routed_block(jax.random.fold_in(splits[2], 2), own, number, TOK_EP, EXPERTS, TOP, CAP, 2))(routes_keys, routes_turns).reshape((TOKENS, TOP))
    gates = jnp.clip(0.1 + 0.5 * jax.random.uniform(splits[3], (TOKENS, TOP), jnp.float32) ** block_scale(splits[3], (TOKENS, TOP), ((0, 32),), -0.2, 0.2), 0.1, 0.6)
    expert_gate = bell_draw(splits[4], (EXPERTS, D_T, FE), D_T ** -0.5, 0.0625, ((0, 32), (2, 4)))
    expert_up = bell_draw(splits[5], (EXPERTS, D_T, FE), D_T ** -0.5, 0.0625, ((0, 32), (2, 4)))
    expert_down = bell_draw(splits[6], (EXPERTS, FE, D_T), FE ** -0.5, 0.1875, ((0, 32), (1, 4)))
    projection = bell_draw(splits[7], (D_T, D_S), D_T ** -0.5, 0.0625, ((1, 128),))
    student_in = bell_draw(splits[8], (TOKENS, D_S), 1.0, 6.0, ((1, 128),))
    student_gain = jnp.clip(1.0 + 0.1 * jax.random.normal(splits[9], (D_S,), jnp.float32), 0.5, 1.5)
    student_gate = bell_draw(splits[10], (D_S, FF), D_S ** -0.5, 0.0625, ((1, 128),))
    student_up = bell_draw(splits[11], (D_S, FF), D_S ** -0.5, 0.0625, ((1, 128),))
    student_down = noise_with(splits[12], (FF, D_S), FF ** -0.5, 0.1875, ((0, 128),), (0, 1, 128, 5.5))
    return {"teacher_in": teacher_in, "teacher_gain": teacher_gain, "routes": routes, "gates": gates, "expert_gate": expert_gate, "expert_up": expert_up, "expert_down": expert_down, "projection": projection, "student_in": student_in, "student_gain": student_gain, "student_gate": student_gate, "student_up": student_up, "student_down": student_down}


def rms_norm(values, scale_gain):
    floats = values.astype(jnp.float32)
    factor = lax.rsqrt(lax.optimization_barrier(jnp.mean(floats * floats, axis=-1, keepdims=True)) + 1e-05)
    return (floats * factor * scale_gain).astype(jnp.bfloat16)

def reference(teacher_in, teacher_gain, routes, gates, expert_gate, expert_up, expert_down, projection, student_in, student_gain, student_gate, student_up, student_down):
    quarters = N_GRP * N_REP
    quarter_width = FE // quarters
    most_rows = N_EP * CAP
    teacher_normed = rms_norm(teacher_in, teacher_gain)

    def one_expert(moe_sum, expert_id):
        hits = routes == expert_id
        route_weight = lax.optimization_barrier(jnp.sum(jnp.where(hits, gates, 0.0), axis=1))
        token_index = jnp.nonzero(jnp.any(hits, axis=1), size=most_rows, fill_value=0)[0].astype(jnp.int32)
        is_valid = jnp.arange(most_rows) < jnp.sum(jnp.any(hits, axis=1).astype(jnp.int32))
        routed_rows = teacher_normed[token_index]
        weight_rows = jnp.where(is_valid, route_weight[token_index], 0.0)
        w_gate = lax.dynamic_index_in_dim(expert_gate, expert_id, 0, keepdims=False)
        w_up = lax.dynamic_index_in_dim(expert_up, expert_id, 0, keepdims=False)
        w_down = lax.dynamic_index_in_dim(expert_down, expert_id, 0, keepdims=False)
        gathered_out = jnp.zeros((most_rows, D_T), jnp.float32)
        for quarter in range(quarters):
            low = quarter * quarter_width
            gate_pre = jnp.dot(routed_rows, w_gate[:, low:low + quarter_width], preferred_element_type=jnp.float32)
            up_pre = jnp.dot(routed_rows, w_up[:, low:low + quarter_width], preferred_element_type=jnp.float32)
            hidden = (jax.nn.silu(gate_pre) * up_pre).astype(jnp.bfloat16)
            out_q = jnp.dot(hidden, w_down[low:low + quarter_width, :], preferred_element_type=jnp.float32).astype(jnp.bfloat16)
            out_q = lax.optimization_barrier(out_q).astype(jnp.float32)
            gathered_out = gathered_out + out_q * weight_rows[:, None]
        moe_sum = moe_sum.at[token_index].add(gathered_out)
        return (moe_sum, None)
    moe, _ = lax.scan(one_expert, jnp.zeros((TOKENS, D_T), jnp.float32), jnp.arange(EXPERTS, dtype=jnp.int32))
    teacher_out = (teacher_in.astype(jnp.float32) + moe).astype(jnp.bfloat16)
    target = jnp.dot(teacher_out, projection, preferred_element_type=jnp.float32)
    student_normed = rms_norm(student_in, student_gain)
    gate_pre = jnp.dot(student_normed, student_gate, preferred_element_type=jnp.float32)
    up_pre = jnp.dot(student_normed, student_up, preferred_element_type=jnp.float32)
    act = (jax.nn.silu(gate_pre) * up_pre).astype(jnp.bfloat16)
    student_out = student_in.astype(jnp.float32) + jnp.dot(act, student_down, preferred_element_type=jnp.float32)
    diff = student_out - target
    mse = jnp.mean(diff * diff)
    delta = (diff / math.sqrt(TOKENS)).astype(jnp.bfloat16)
    grad_down = jnp.dot(act.T, delta, preferred_element_type=jnp.float32).astype(jnp.bfloat16)
    back_act = jnp.dot(delta, student_down.T, preferred_element_type=jnp.float32)
    sigmoid_g = jax.nn.sigmoid(gate_pre)
    d_gate = (back_act * up_pre * sigmoid_g * (1.0 + gate_pre * (1.0 - sigmoid_g))).astype(jnp.bfloat16)
    d_up = (back_act * gate_pre * sigmoid_g).astype(jnp.bfloat16)
    grad_gate = jnp.dot(student_normed.T, d_gate, preferred_element_type=jnp.float32).astype(jnp.bfloat16)
    grad_up = jnp.dot(student_normed.T, d_up, preferred_element_type=jnp.float32).astype(jnp.bfloat16)
    return (grad_gate, grad_up, grad_down, mse)
```

```python
import math

import jax
import jax.numpy as jnp
from jax import lax
from jax.experimental import pallas as pl
from jax.experimental.pallas import tpu as pltpu
from jax.sharding import PartitionSpec as P

CHIPS = ("grp", "ep")
NN = (((1,), (0,)), ((), ()))
NT = (((1,), (1,)), ((), ()))
TN = (((0,), (0,)), ((), ()))
VMEM_BYTES = 56 * 1024 * 1024


def dot(a, b, dims=NN):
    return lax.dot_general(a, b, dims, preferred_element_type=jnp.float32)


def silu(v):
    return v / (1.0 + jnp.exp(-v))


def params():
    return pltpu.CompilerParams(vmem_limit_bytes=VMEM_BYTES)


def vmem():
    return pl.BlockSpec(memory_space=pltpu.VMEM)


def anywhere():
    return pl.BlockSpec(memory_space=pl.ANY)


def exchange(blocks):
    return lax.all_to_all(blocks, CHIPS, split_axis=0, concat_axis=0, tiled=True)


def spread(block):
    chips = lax.axis_size(CHIPS)
    return exchange(jnp.broadcast_to(block[None], (chips,) + block.shape))


def other_core(values):
    return lax.ppermute(values, "rep", [(0, 1), (1, 0)])


def expert_kernel(
    mine, other, gain, weight, gate_hbm, up_hbm, down_hbm, keep, send, gate_w, up_w, down_w, sems
):
    half = mine.shape[1]
    core = lax.axis_index("rep")
    first = pl.multiple_of(core * half, half)
    second = pl.multiple_of((1 - core) * half, half)
    copies = []
    for n, start in enumerate((first, second)):
        rows = pl.ds(start, half)
        for m, (src, dst) in enumerate(((gate_hbm, gate_w), (up_hbm, up_w))):
            copies.append(pltpu.make_async_copy(src.at[rows], dst.at[n], sems.at[2 * n + m]))
    copies.append(pltpu.make_async_copy(down_hbm, down_w, sems.at[4]))
    for copy in copies:
        copy.start()
    floats = [mine[...].astype(jnp.float32), other[...].astype(jnp.float32)]
    squares = sum(jnp.sum(v * v, axis=1, keepdims=True) for v in floats)
    factor = lax.rsqrt(squares / (2 * half) + 1e-05)
    gains = [gain[pl.ds(core, 1), :], gain[pl.ds(1 - core, 1), :]]
    normed = [(v * factor * g).astype(jnp.bfloat16) for v, g in zip(floats, gains)]
    copies[0].wait()
    gate_pre = dot(normed[0], gate_w[0])
    copies[1].wait()
    up_pre = dot(normed[0], up_w[0])
    copies[2].wait()
    gate_pre += dot(normed[1], gate_w[1])
    copies[3].wait()
    up_pre += dot(normed[1], up_w[1])
    hidden = (silu(gate_pre) * up_pre).astype(jnp.bfloat16)
    copies[4].wait()
    scale = weight[...]
    is_first = (lax.axis_index("grp") == 0) & (lax.axis_index("ep") == 0)
    own = jnp.where(is_first, 1.0, 0.0)
    width = 512
    for n in range(half // width):
        here = slice(n * width, (n + 1) * width)
        columns = pl.ds(pl.multiple_of(second + n * width, width), width)
        out = dot(hidden, down_w[:, columns]) * scale
        send[here, :] = out.T.astype(jnp.bfloat16)
    for n in range(half // width):
        here = slice(n * width, (n + 1) * width)
        columns = pl.ds(pl.multiple_of(first + n * width, width), width)
        out = dot(hidden, down_w[:, columns]) * scale
        out += mine[:, here].astype(jnp.float32) * own
        keep[here, :] = out.T


def experts(mine, other, gain, weight, w_gate, w_up, w_down):
    tokens, half = mine.shape
    hidden = w_gate.shape[1]
    return pl.pallas_call(
        expert_kernel,
        out_shape=(
            jax.ShapeDtypeStruct((half, tokens), jnp.float32),
            jax.ShapeDtypeStruct((half, tokens), jnp.bfloat16),
        ),
        in_specs=[vmem()] * 4 + [anywhere()] * 3,
        out_specs=(vmem(), vmem()),
        scratch_shapes=[
            pltpu.VMEM((2, half, hidden), jnp.bfloat16),
            pltpu.VMEM((2, half, hidden), jnp.bfloat16),
            pltpu.VMEM((hidden, 2 * half), jnp.bfloat16),
            pltpu.SemaphoreType.DMA((5,)),
        ],
        compiler_params=params(),
        name="experts",
    )(mine, other, gain, weight, w_gate, w_up, w_down)


def prepare_kernel(gate, up, gain, scaled):
    rows = gate.shape[0]
    scaled[:rows, :] = (gate[...].astype(jnp.float32) * gain[...]).astype(jnp.bfloat16)
    scaled[rows:, :] = (up[...].astype(jnp.float32) * gain[...]).astype(jnp.bfloat16)


def prepare(gate, up, gain):
    rows, width = gate.shape
    return pl.pallas_call(
        prepare_kernel,
        out_shape=jax.ShapeDtypeStruct((2 * rows, width), jnp.bfloat16),
        in_specs=[vmem()] * 3,
        out_specs=vmem(),
        compiler_params=params(),
        name="prepare",
    )(gate, up, gain)


def start_interleaved(mine, other, dst, sems):
    core = lax.axis_index("rep")
    copies = [
        pltpu.make_async_copy(mine, dst.at[:, core], sems.at[0]),
        pltpu.make_async_copy(other, dst.at[:, 1 - core], sems.at[1]),
    ]
    for copy in copies:
        copy.start()
    return copies


def forward_kernel(mine, other, scaled, down, keep, send, act_ref, pre_ref, factor_ref, x, sems):
    core = lax.axis_index("rep")
    chips, _, rows, tokens = x.shape
    features = chips * 2 * rows
    for copy in start_interleaved(mine, other, x, sems):
        copy.wait()
    values = x[...].reshape(features, tokens)
    floats = values.astype(jnp.float32)
    factor = lax.rsqrt(jnp.sum(floats * floats, axis=0, keepdims=True) / features + 1e-05)
    factor_ref[...] = factor
    pre = dot(scaled[...], values) * factor
    pre_ref[...] = pre
    hidden = pre.shape[0] // 2
    act = (silu(pre[:hidden]) * pre[hidden:]).astype(jnp.bfloat16)
    act_ref[...] = act
    step = 8
    width = step * 2 * rows
    for n in range(chips // step):
        part = dot(down[:, n * width : (n + 1) * width], act, TN).reshape(step, 2, rows, tokens)
        here = slice(n * step, (n + 1) * step)
        low, high = part[:, 0], part[:, 1]
        keep[here] = jnp.where(core == 0, low, high)
        send[here] = jnp.where(core == 0, high, low).astype(jnp.bfloat16)


def forward(mine, other, scaled, down):
    chips, rows, tokens = mine.shape
    hidden = down.shape[0]
    return pl.pallas_call(
        forward_kernel,
        out_shape=(
            jax.ShapeDtypeStruct((chips, rows, tokens), jnp.float32),
            jax.ShapeDtypeStruct((chips, rows, tokens), jnp.bfloat16),
            jax.ShapeDtypeStruct((hidden, tokens), jnp.bfloat16),
            jax.ShapeDtypeStruct((2 * hidden, tokens), jnp.float32),
            jax.ShapeDtypeStruct((1, tokens), jnp.float32),
        ),
        in_specs=[anywhere()] * 2 + [vmem()] * 2,
        out_specs=(vmem(),) * 5,
        scratch_shapes=[
            pltpu.VMEM((chips, 2, rows, tokens), jnp.bfloat16),
            pltpu.SemaphoreType.DMA((2,)),
        ],
        compiler_params=params(),
        name="forward",
    )(mine, other, scaled, down)


def delta_kernel(mine, other, projection, partials, student_in, delta):
    core = lax.axis_index("rep")
    half, tokens = mine.shape
    first = pl.multiple_of(core * half, half)
    second = pl.multiple_of((1 - core) * half, half)
    target = dot(projection[:, pl.ds(first, half)], mine[...])
    target += dot(projection[:, pl.ds(second, half)], other[...])
    branch = jnp.sum(partials[...].astype(jnp.float32), axis=0)
    diff = student_in[...].astype(jnp.float32) + branch - target
    scaled = (diff / math.sqrt(tokens)).astype(jnp.bfloat16)
    delta[...] = jnp.broadcast_to(scaled[None], delta.shape)


def deltas(mine, other, projection, partials, student_in):
    return pl.pallas_call(
        delta_kernel,
        out_shape=jax.ShapeDtypeStruct(partials.shape, jnp.bfloat16),
        in_specs=[vmem()] * 5,
        out_specs=vmem(),
        compiler_params=params(),
        name="deltas",
    )(mine, other, projection, partials, student_in)


def backward_kernel(
    d_mine,
    d_other,
    x_mine,
    x_other,
    down,
    act,
    pre,
    factor,
    gain,
    grad_gate,
    grad_up,
    grad_down,
    mse,
    d,
    x,
    sems_d,
    sems_x,
):
    chips, _, rows, tokens = x.shape
    features = chips * 2 * rows
    copies_d = start_interleaved(d_mine, d_other, d, sems_d)
    copies_x = start_interleaved(x_mine, x_other, x, sems_x)
    for copy in copies_d:
        copy.wait()
    hidden = act.shape[0]
    delta = d[...].reshape(features, tokens)
    back = dot(down[...], delta)
    gate_pre, up_pre = pre[:hidden], pre[hidden:]
    sigmoid = 1.0 / (1.0 + jnp.exp(-gate_pre))
    d_gate = back * up_pre * sigmoid * (1.0 + gate_pre * (1.0 - sigmoid))
    d_up = back * gate_pre * sigmoid
    scale = factor[...]
    d_both = jnp.concatenate([d_gate * scale, d_up * scale], axis=0).astype(jnp.bfloat16)
    step = 8
    width = step * 2 * rows
    acts = act[...]
    total = jnp.zeros((1, tokens), jnp.float32)
    for n in range(chips // step):
        here = slice(n * width, (n + 1) * width)
        part = d[n * step : (n + 1) * step].reshape(width, tokens)
        grad_down[:, here] = dot(acts, part, NT).astype(jnp.bfloat16)
        floats = part.astype(jnp.float32)
        total += jnp.sum(floats * floats, axis=0, keepdims=True)
    mse[...] = jnp.sum(total, axis=1, keepdims=True) / features
    for copy in copies_x:
        copy.wait()
    for n in range(chips // step):
        here = slice(n * width, (n + 1) * width)
        part = x[n * step : (n + 1) * step].reshape(width, tokens)
        grads = dot(d_both, part, NT) * gain[:, here]
        grad_gate[:, here] = grads[:hidden].astype(jnp.bfloat16)
        grad_up[:, here] = grads[hidden:].astype(jnp.bfloat16)


def backward(d_mine, d_other, x_mine, x_other, down, act, pre, factor, gain):
    chips, rows, tokens = d_mine.shape
    hidden, features = down.shape
    grad = jax.ShapeDtypeStruct((hidden, features), jnp.bfloat16)
    whole = pltpu.VMEM((chips, 2, rows, tokens), jnp.bfloat16)
    return pl.pallas_call(
        backward_kernel,
        out_shape=(grad, grad, grad, jax.ShapeDtypeStruct((1, 1), jnp.float32)),
        in_specs=[anywhere()] * 4 + [vmem()] * 5,
        out_specs=(vmem(),) * 4,
        scratch_shapes=[
            whole,
            whole,
            pltpu.SemaphoreType.DMA((2,)),
            pltpu.SemaphoreType.DMA((2,)),
        ],
        compiler_params=params(),
        name="backward",
    )(d_mine, d_other, x_mine, x_other, down, act, pre, factor, gain)


def local(
    teacher_in,
    teacher_gain,
    routes,
    gates,
    expert_gate,
    expert_up,
    expert_down,
    projection,
    student_in,
    student_gain,
    student_gate,
    student_up,
    student_down,
):
    groups, experts_in_all, cores = (lax.axis_size(a) for a in ("grp", "ep", "rep"))
    chips = groups * experts_in_all
    group, expert, core = (lax.axis_index(a) for a in ("grp", "ep", "rep"))
    rows_here, model_width = teacher_in.shape
    tokens = rows_here * experts_in_all
    quarter = model_width // (groups * cores)
    lanes = 128

    ids = jnp.arange(experts_in_all, dtype=jnp.int32)
    weights = jnp.sum(
        jnp.where(routes[:, :, None] == ids[None, None, :], gates[:, :, None], 0.0), axis=1
    )
    weights_high = lax.reduce_precision(weights, exponent_bits=8, mantissa_bits=7)
    weights_low = weights - weights_high
    both = jnp.stack([weights_high, weights_low]).astype(jnp.bfloat16).reshape(2, lanes)
    part = lax.dynamic_slice_in_dim(teacher_in, (core * groups + group) * quarter, quarter, axis=1)
    data_rows = rows_here * quarter // lanes
    block = jnp.concatenate([part.reshape(data_rows, lanes), both], axis=0)
    block = jnp.pad(block, ((0, 64 - block.shape[0]), (0, 0)))
    arrived = spread(block)
    arrived_other = other_core(arrived)

    def tokens_of(blocks):
        cut = blocks[:, :data_rows].reshape(groups, experts_in_all, rows_here, quarter)
        return cut.transpose(1, 2, 0, 3).reshape(tokens, groups * quarter)

    weight_rows = arrived[:experts_in_all, data_rows : data_rows + 2].astype(jnp.float32)
    weight_all = weight_rows.sum(axis=1).reshape(tokens, experts_in_all)
    weight_here = lax.dynamic_slice_in_dim(weight_all, expert, 1, axis=1)
    keep, send = experts(
        tokens_of(arrived),
        tokens_of(arrived_other),
        teacher_gain.reshape(cores, -1),
        weight_here,
        expert_gate[0],
        expert_up[0],
        expert_down[0],
    )
    moe = (keep + other_core(send).astype(jnp.float32)).astype(jnp.bfloat16)
    moe = exchange(moe.reshape(chips, -1, tokens))
    teacher_out = jnp.sum(moe.astype(jnp.float32), axis=0).astype(jnp.bfloat16)
    teacher_mine = spread(teacher_out)
    teacher_other = other_core(teacher_mine)

    student_t = student_in.T
    gain_row = student_gain[None, :]
    scaled = prepare(student_gate.T, student_up.T, gain_row)
    x_mine = spread(student_t)
    x_other = other_core(x_mine)
    s_keep, s_send, act, pre, factor = forward(x_mine, x_other, scaled, student_down)
    sums = (s_keep + other_core(s_send).astype(jnp.float32)).astype(jnp.bfloat16)
    partials = exchange(sums)

    delta = deltas(
        teacher_mine.reshape(-1, tokens),
        teacher_other.reshape(-1, tokens),
        projection.T,
        partials,
        student_t,
    )
    d_mine = exchange(delta)
    d_other = other_core(d_mine)
    grad_gate, grad_up, grad_down, mse = backward(
        d_mine, d_other, x_mine, x_other, student_down, act, pre, factor, gain_row
    )
    return (grad_gate.T, grad_up.T, grad_down, mse.reshape(()))


def solution(mesh):
    everything = ("grp", "ep", "rep")
    placed = (
        P("ep", None),
        P(),
        P("ep", None),
        P("ep", None),
        P("ep", None, ("grp", "rep")),
        P("ep", None, ("grp", "rep")),
        P("ep", ("grp", "rep"), None),
        P(None, everything),
        P(None, everything),
        P(),
        P(None, everything),
        P(None, everything),
        P(everything, None),
    )
    return jax.shard_map(
        local,
        mesh=mesh,
        in_specs=placed,
        out_specs=(P(None, everything), P(None, everything), P(everything, None), P()),
        check_vma=False,
    )
```

```python
import math

import jax
import jax.numpy as jnp
from jax import lax
from jax.experimental import pallas as pl
from jax.experimental.pallas import tpu as pltpu
from jax.sharding import PartitionSpec as P

CHIPS = ("grp", "ep")
NN = (((1,), (0,)), ((), ()))
NT = (((1,), (1,)), ((), ()))
TN = (((0,), (0,)), ((), ()))
LANES = 128


def dot(a, b, dims=NN):
    return lax.dot_general(a, b, dims, preferred_element_type=jnp.float32)


def silu(v):
    return v / (1.0 + jnp.exp(-v))


def params(mebibytes):
    return pltpu.CompilerParams(vmem_limit_bytes=mebibytes * 1024 * 1024)


def cost(microseconds):
    size = int(microseconds * 3e6)
    return pl.CostEstimate(flops=0, bytes_accessed=size, transcendentals=0)


def vmem():
    return pl.BlockSpec(memory_space=pltpu.VMEM)


def anywhere():
    return pl.BlockSpec(memory_space=pl.ANY)


def exchange(blocks):
    return lax.all_to_all(blocks, CHIPS, split_axis=0, concat_axis=0, tiled=True)


def other_core(values):
    return lax.ppermute(values, "rep", [(0, 1), (1, 0)])


def slot_weights(routes, gates, experts, copies):
    tokens, _ = routes.shape
    row = lax.broadcasted_iota(jnp.int32, (copies * experts * 2, routes.shape[1]), 0)
    expert, slot = (row // 2) % experts, (row % 2)[:, :1]
    earlier = jnp.zeros(slot.shape, jnp.float32)
    weights = []
    for t in range(tokens):
        hits = routes[t : t + 1, :] == expert
        taken = jnp.sum(jnp.where(hits, 1.0, 0.0), axis=1, keepdims=True)
        value = jnp.sum(jnp.where(hits, gates[t : t + 1, :], 0.0), axis=1, keepdims=True)
        weights.append(jnp.where(earlier == slot.astype(jnp.float32), value, 0.0))
        earlier += taken
    return weights


def padded_pieces(pieces):
    return -(-pieces // 8) * 8


def dispatch_kernel(tokens_hbm, routes_hbm, student_hbm, out, rows, tokens, routes, student, sems):
    pairs = ((routes_hbm, routes), (tokens_hbm, tokens), (student_hbm, student))
    copies_in = [pltpu.make_async_copy(a, b, sems.at[n]) for n, (a, b) in enumerate(pairs)]
    for copy in copies_in:
        copy.start()
    for copy in copies_in:
        copy.wait()
    copies = lax.axis_size("grp")
    experts = lax.axis_size("ep")
    quarter = tokens.shape[1] // (copies * lax.axis_size("rep"))
    place = lax.axis_index("rep") * copies + lax.axis_index("grp")
    start = pl.multiple_of(place * quarter, quarter)
    ids = routes[...]
    chosen = slot_weights(ids, jnp.ones(ids.shape, jnp.float32), experts, 1)
    pieces = quarter // LANES
    stride = padded_pieces(pieces)
    rows[...] = jnp.zeros(rows.shape, jnp.float32)
    for n in range(pieces):
        values = tokens[:, pl.ds(start + n * LANES, LANES)].astype(jnp.float32)
        picked = sum(c * values[t : t + 1, :] for t, c in enumerate(chosen))
        rows[pl.ds(n, 2 * experts, stride=stride), :] = picked
    here = student.shape[0]
    routed = rows[...].astype(jnp.bfloat16).reshape(experts, 2 * stride, LANES)
    for n in range(copies):
        out[n * experts : (n + 1) * experts, here:, :] = routed
    block = student[...]
    out[:, :here, :] = jnp.broadcast_to(block[None], (out.shape[0],) + block.shape)


def dispatch(tokens, routes, student):
    copies, experts = lax.axis_size("grp"), lax.axis_size("ep")
    rows = 2 * padded_pieces(tokens.shape[1] // (copies * lax.axis_size("rep") * LANES))
    shape = (copies * experts, student.shape[0] + rows, LANES)
    return pl.pallas_call(
        dispatch_kernel,
        out_shape=jax.ShapeDtypeStruct(shape, jnp.bfloat16),
        in_specs=[anywhere()] * 3,
        out_specs=vmem(),
        scratch_shapes=[
            pltpu.VMEM((experts * rows, LANES), jnp.float32),
            pltpu.VMEM(tokens.shape, tokens.dtype),
            pltpu.VMEM(routes.shape, routes.dtype),
            pltpu.VMEM(student.shape, student.dtype),
            pltpu.SemaphoreType.DMA((3,)),
        ],
        compiler_params=params(8),
        cost_estimate=cost(2),
        name="dispatch",
    )(tokens, routes, student)


def expert_kernel(
    mine,
    other,
    gain,
    gate_w,
    up_w,
    down_w,
    keep,
    send,
    rows,
    normed,
    result,
):
    half = gain.shape[1] // 2
    groups = lax.axis_size("grp")
    pieces = half // (groups * LANES)
    routed = rows.shape[1]
    stride = padded_pieces(pieces)
    slots = routed // (groups * stride)
    core = lax.axis_index("rep")
    first = pl.multiple_of(core * half, half)
    second = pl.multiple_of((1 - core) * half, half)
    squares = jnp.zeros((slots, LANES), jnp.float32)
    for n, source in enumerate((mine, other)):
        rows[n] = source[...].astype(jnp.float32).reshape(routed, LANES)
        for g in range(groups):
            for m in range(pieces):
                values = rows[n, pl.ds(g * slots * stride + m, slots, stride=stride), :]
                squares += values * values
    factor = lax.rsqrt(jnp.sum(squares, axis=1, keepdims=True) / (2 * half) + 1e-05)
    factor = jnp.broadcast_to(factor, (slots, LANES))
    for n in range(2):
        gains = gain[:, pl.ds((first, second)[n], half)]
        for g in range(groups):
            for m in range(pieces):
                column = (g * pieces + m) * LANES
                columns = slice(column, column + LANES)
                values = rows[n, pl.ds(g * slots * stride + m, slots, stride=stride), :]
                values = values * factor * gains[:, columns]
                normed[n, :, columns] = values.astype(jnp.bfloat16)
    gate_pre = dot(normed[0], gate_w[pl.ds(first, half), :])
    up_pre = dot(normed[0], up_w[pl.ds(first, half), :])
    gate_pre += dot(normed[1], gate_w[pl.ds(second, half), :])
    up_pre += dot(normed[1], up_w[pl.ds(second, half), :])
    hidden = (silu(gate_pre) * up_pre).astype(jnp.bfloat16)
    parts = pieces
    width = half // 2
    result[...] = jnp.zeros(result.shape, jnp.float32)
    for dst, start in ((send, second), (keep, first)):
        for n in range(2):
            columns = pl.ds(pl.multiple_of(start + n * width, width), width)
            out = dot(hidden, down_w[:, columns])
            for m in range(parts):
                place = pl.ds(n * slots * stride + m, slots, stride=stride)
                result[place, :] = out[:, m * LANES : (m + 1) * LANES]
        dst[...] = result[...].astype(dst.dtype)


def experts(mine, other, gain, w_gate, w_up, w_down):
    groups, count = lax.axis_size("grp"), lax.axis_size("ep")
    half = gain.shape[1] // 2
    slots = 2 * count
    result = (groups * slots * padded_pieces(half // (groups * LANES)), LANES)
    return pl.pallas_call(
        expert_kernel,
        out_shape=(
            jax.ShapeDtypeStruct(result, jnp.float32),
            jax.ShapeDtypeStruct(result, jnp.bfloat16),
        ),
        in_specs=[vmem()] * 6,
        out_specs=(vmem(),) * 2,
        scratch_shapes=[
            pltpu.VMEM((2,) + result, jnp.float32),
            pltpu.VMEM((2, slots, half), jnp.bfloat16),
            pltpu.VMEM(result, jnp.float32),
        ],
        compiler_params=params(10),
        cost_estimate=cost(3),
        name="experts",
    )(mine, other, gain, w_gate, w_up, w_down)


def combine_kernel(returned, tokens, routes, gates, keep, received, out, rows, own):
    copies = lax.axis_size("grp")
    experts = lax.axis_size("ep")
    slots = 2 * copies * experts
    stride = returned.shape[0] // slots
    quarter = tokens.shape[1] // (copies * lax.axis_size("rep"))
    pieces = quarter // LANES
    place = lax.axis_index("rep") * copies + lax.axis_index("grp")
    start = pl.multiple_of(place * quarter, quarter)
    count = tokens.shape[0]
    weights = slot_weights(routes[...], gates[...], experts, copies)
    weights = [jnp.broadcast_to(w, (slots, LANES)) for w in weights]
    rows[...] = returned[...].astype(jnp.float32)
    for m in range(pieces):
        values = rows[pl.ds(m, slots, stride=stride), :]
        before = tokens[:, pl.ds(start + m * LANES, LANES)].astype(jnp.float32)
        for t in range(count):
            moe = jnp.sum(values * weights[t], axis=0, keepdims=True)
            own[t * pieces + m : t * pieces + m + 1, :] = before[t : t + 1, :] + moe
    here = keep.shape[1]
    block = own[...].astype(jnp.bfloat16)
    out[:, :here, :] = (keep[...] + received[...].astype(jnp.float32)).astype(jnp.bfloat16)
    out[:, here:, :] = jnp.broadcast_to(block[None], (out.shape[0],) + block.shape)


def combine(returned, tokens, routes, gates, keep, received):
    chips, rows, _ = keep.shape
    own = tokens.size // (lax.axis_size("grp") * lax.axis_size("rep") * LANES)
    return pl.pallas_call(
        combine_kernel,
        out_shape=jax.ShapeDtypeStruct((chips, rows + own, LANES), jnp.bfloat16),
        in_specs=[vmem()] * 6,
        out_specs=vmem(),
        scratch_shapes=[
            pltpu.VMEM(returned.shape, jnp.float32),
            pltpu.VMEM((own, LANES), jnp.float32),
        ],
        compiler_params=params(16),
        cost_estimate=cost(4),
        name="combine",
    )(returned, tokens, routes, gates, keep, received)


def split_kernel(arrived, student, routed):
    rows = student.shape[1]
    routed[...] = arrived[:, rows:, :]
    student[...] = arrived[:, :rows, :]


def split(arrived, rows):
    chips, total, lanes = arrived.shape
    return pl.pallas_call(
        split_kernel,
        out_shape=(
            jax.ShapeDtypeStruct((chips, rows, lanes), arrived.dtype),
            jax.ShapeDtypeStruct((chips, total - rows, lanes), arrived.dtype),
        ),
        in_specs=[vmem()],
        out_specs=(vmem(),) * 2,
        compiler_params=params(4),
        cost_estimate=cost(1),
        name="split",
    )(arrived)


def fetch_kernel(up_hbm, down_hbm, projection, after, up, down, cut, sems):
    half = cut.shape[1]
    start = pl.multiple_of((1 - lax.axis_index("rep")) * half, half)
    pairs = ((up_hbm, up), (down_hbm, down), (projection.at[:, pl.ds(start, half)], cut))
    copies = [pltpu.make_async_copy(a, b, sems.at[n]) for n, (a, b) in enumerate(pairs)]
    for copy in copies:
        copy.start()
    for copy in copies:
        copy.wait()


def fetch(up, down, projection, after):
    rows, width = projection.shape
    return pl.pallas_call(
        fetch_kernel,
        out_shape=(
            pltpu.VMEM(up.shape, up.dtype),
            pltpu.VMEM(down.shape, down.dtype),
            jax.ShapeDtypeStruct((rows, width // 2), projection.dtype),
        ),
        in_specs=[anywhere()] * 4,
        out_specs=(vmem(),) * 3,
        scratch_shapes=[pltpu.SemaphoreType.DMA((3,))],
        compiler_params=params(4),
        cost_estimate=cost(4),
        name="fetch",
    )(up, down, projection, after)


def merge_kernel(keep, received, after, out):
    out[...] = (keep[...] + received[...].astype(jnp.float32)).astype(out.dtype)


def merge(keep, received, after):
    return pl.pallas_call(
        merge_kernel,
        out_shape=jax.ShapeDtypeStruct(received.shape, received.dtype),
        in_specs=[vmem()] * 2 + [anywhere()],
        out_specs=vmem(),
        compiler_params=params(6),
        cost_estimate=cost(1),
        name="merge",
    )(keep, received, after)


def start_interleaved(mine, other, dst, sems):
    core = lax.axis_index("rep")
    copies = [
        pltpu.make_async_copy(mine, dst.at[:, core], sems.at[0]),
        pltpu.make_async_copy(other, dst.at[:, 1 - core], sems.at[1]),
    ]
    for copy in copies:
        copy.start()
    return copies


def forward_kernel(mine, other, gate_hbm, up_hbm, down_hbm, gain, after, keep, *refs):
    send, act_ref, pre_ref, factor_ref, x, raw, scaled, down, sems, sems_x = refs
    core = lax.axis_index("rep")
    chips, cores, rows, tokens = x.shape
    features = chips * cores * rows
    hidden = down.shape[0]
    copies = [
        pltpu.make_async_copy(gate_hbm, raw.at[0], sems.at[0]),
        pltpu.make_async_copy(up_hbm, raw.at[1], sems.at[1]),
        pltpu.make_async_copy(down_hbm, down, sems.at[2]),
    ]
    for copy in copies:
        copy.start()
    copies_x = start_interleaved(mine, other, x, sems_x)
    for n in range(2):
        copies[n].wait()
        part = (raw[n].astype(jnp.float32) * gain[...]).astype(jnp.bfloat16)
        scaled[n * hidden : (n + 1) * hidden, :] = part
    for copy in copies_x:
        copy.wait()
    values = x[...].reshape(features, tokens)
    floats = values.astype(jnp.float32)
    factor = lax.rsqrt(jnp.sum(floats * floats, axis=0, keepdims=True) / features + 1e-05)
    factor_ref[...] = factor
    pre = dot(scaled[...], values) * factor
    pre_ref[...] = pre
    act = (silu(pre[:hidden]) * pre[hidden:]).astype(jnp.bfloat16)
    act_ref[...] = act
    copies[2].wait()
    step = 8
    width = step * 2 * rows
    for n in range(chips // step):
        part = dot(down[:, n * width : (n + 1) * width], act, TN).reshape(step, 2, rows, tokens)
        here = slice(n * step, (n + 1) * step)
        low, high = part[:, 0], part[:, 1]
        keep[here] = jnp.where(core == 0, low, high)
        send[here] = jnp.where(core == 0, high, low).astype(jnp.bfloat16)


def forward(mine, other, gate, up, down, gain, after):
    chips, _, tokens = mine.shape
    hidden, features = down.shape
    rows = features // (2 * chips)
    whole = (chips, 2, rows, tokens)
    return pl.pallas_call(
        forward_kernel,
        out_shape=(
            jax.ShapeDtypeStruct((chips, rows, tokens), jnp.float32),
            jax.ShapeDtypeStruct((chips, rows, tokens), jnp.bfloat16),
            jax.ShapeDtypeStruct((hidden, tokens), jnp.bfloat16),
            jax.ShapeDtypeStruct((2 * hidden, tokens), jnp.float32),
            jax.ShapeDtypeStruct((1, tokens), jnp.float32),
            jax.ShapeDtypeStruct(whole, jnp.bfloat16),
        ),
        in_specs=[anywhere()] * 5 + [vmem(), anywhere()],
        out_specs=(vmem(),) * 6,
        scratch_shapes=[
            pltpu.VMEM((2, hidden, features), jnp.bfloat16),
            pltpu.VMEM((2 * hidden, features), jnp.bfloat16),
            pltpu.VMEM((hidden, features), jnp.bfloat16),
            pltpu.SemaphoreType.DMA((3,)),
            pltpu.SemaphoreType.DMA((2,)),
        ],
        compiler_params=params(28),
        cost_estimate=cost(2),
        name="forward",
    )(mine, other, gate, up, down, gain, after)


def target_kernel(arrived, projection, projection_other, student_in, near, far, rows, tokens):
    here = student_in.shape[0]
    chips, total, lanes = arrived.shape
    count, half = tokens.shape
    groups = lax.axis_size("grp")
    pieces = half // (groups * lanes)
    start = pl.multiple_of(lax.axis_index("rep") * half, half)
    rows[...] = arrived[:, here:, :].astype(jnp.float32).reshape(rows.shape)
    for g in range(groups):
        for m in range(pieces):
            place = pl.ds(g * count * pieces + m, count, stride=pieces)
            columns = slice((g * pieces + m) * lanes, (g * pieces + m + 1) * lanes)
            tokens[:, columns] = rows[place, :].astype(jnp.bfloat16)
    values = tokens[...]
    far[...] = dot(projection_other[...], values, NT)
    branch = jnp.sum(arrived[:, :here, :].astype(jnp.float32), axis=0)
    target = dot(projection[:, pl.ds(start, half)], values, NT)
    near[...] = student_in[...].astype(jnp.float32) + branch - target


def targets(arrived, projection, projection_other, student_in):
    here, count = student_in.shape
    chips, total, lanes = arrived.shape
    half = projection_other.shape[1]
    part = jax.ShapeDtypeStruct((here, count), jnp.float32)
    return pl.pallas_call(
        target_kernel,
        out_shape=(part, part),
        in_specs=[vmem()] * 4,
        out_specs=(vmem(),) * 2,
        scratch_shapes=[
            pltpu.VMEM((chips * (total - here), lanes), jnp.float32),
            pltpu.VMEM((count, half), jnp.bfloat16),
        ],
        compiler_params=params(16),
        cost_estimate=cost(4),
        name="targets",
    )(arrived, projection, projection_other, student_in)


def delta_kernel(near, far, delta):
    tokens = near.shape[1]
    scaled = ((near[...] - far[...]) / math.sqrt(tokens)).astype(jnp.bfloat16)
    delta[...] = jnp.broadcast_to(scaled[None], delta.shape)


def deltas(near, far, chips):
    return pl.pallas_call(
        delta_kernel,
        out_shape=jax.ShapeDtypeStruct((chips,) + near.shape, jnp.bfloat16),
        in_specs=[vmem()] * 2,
        out_specs=vmem(),
        compiler_params=params(4),
        cost_estimate=cost(1),
        name="deltas",
    )(near, far)


def backward_kernel(
    d_mine,
    d_other,
    x,
    down,
    act,
    pre,
    factor,
    gain,
    grad_gate_hbm,
    grad_up_hbm,
    grad_down_hbm,
    mse,
    d,
    grad_gate,
    grad_up,
    grad_down,
    sems_d,
    sems_out,
):
    chips, _, rows, tokens = d.shape
    features = chips * 2 * rows
    copies_d = start_interleaved(d_mine, d_other, d, sems_d)
    for copy in copies_d:
        copy.wait()
    hidden = act.shape[0]
    delta = d[...].reshape(features, tokens)
    back = dot(down[...], delta)
    gate_pre, up_pre = pre[:hidden], pre[hidden:]
    sigmoid = 1.0 / (1.0 + jnp.exp(-gate_pre))
    d_gate = back * up_pre * sigmoid * (1.0 + gate_pre * (1.0 - sigmoid))
    d_up = back * gate_pre * sigmoid
    scale = factor[...]
    d_both = jnp.concatenate([d_gate * scale, d_up * scale], axis=0).astype(jnp.bfloat16)
    step = 8
    width = step * 2 * rows
    acts = act[...]
    copies = []

    def send_out(kind, n, src, dst):
        here = slice(n * width, (n + 1) * width)
        copy = pltpu.make_async_copy(src.at[:, here], dst.at[:, here], sems_out.at[kind, n])
        copy.start()
        copies.append(copy)

    total = jnp.zeros((1, tokens), jnp.float32)
    for n in range(chips // step):
        here = slice(n * width, (n + 1) * width)
        part = d[n * step : (n + 1) * step].reshape(width, tokens)
        grad_down[:, here] = dot(acts, part, NT).astype(jnp.bfloat16)
        send_out(0, n, grad_down, grad_down_hbm)
        floats = part.astype(jnp.float32)
        total += jnp.sum(floats * floats, axis=0, keepdims=True)
    mse[...] = jnp.sum(total, axis=1, keepdims=True) / features
    for n in range(chips // step):
        here = slice(n * width, (n + 1) * width)
        part = x[n * step : (n + 1) * step].reshape(width, tokens)
        grads = dot(d_both, part, NT) * gain[:, here]
        grad_gate[:, here] = grads[:hidden].astype(jnp.bfloat16)
        grad_up[:, here] = grads[hidden:].astype(jnp.bfloat16)
        send_out(1, n, grad_gate, grad_gate_hbm)
        send_out(2, n, grad_up, grad_up_hbm)
    for copy in copies:
        copy.wait()


def backward(d_mine, d_other, x, down, act, pre, factor, gain):
    chips, rows, tokens = d_mine.shape
    hidden, features = down.shape
    grad = jax.ShapeDtypeStruct((hidden, features), jnp.bfloat16)
    whole = pltpu.VMEM((chips, 2, rows, tokens), jnp.bfloat16)
    return pl.pallas_call(
        backward_kernel,
        out_shape=(grad, grad, grad, jax.ShapeDtypeStruct((1, 1), jnp.float32)),
        in_specs=[anywhere()] * 2 + [vmem()] * 6,
        out_specs=(anywhere(),) * 3 + (vmem(),),
        scratch_shapes=[
            whole,
            *[pltpu.VMEM((hidden, features), jnp.bfloat16)] * 3,
            pltpu.SemaphoreType.DMA((2,)),
            pltpu.SemaphoreType.DMA((3, 8)),
        ],
        compiler_params=params(24),
        cost_estimate=cost(8),
        name="backward",
    )(d_mine, d_other, x, down, act, pre, factor, gain)


def local(
    teacher_in,
    teacher_gain,
    routes,
    gates,
    expert_gate,
    expert_up,
    expert_down,
    projection,
    student_in,
    student_gain,
    student_gate,
    student_up,
    student_down,
):
    chips = lax.axis_size(CHIPS)
    projection_t = projection.T
    student_t = student_in.T
    gain_row = student_gain[None, :]

    arrived = exchange(dispatch(teacher_in, routes, student_t))
    x_mine, routed = split(arrived, student_t.shape[0])
    routed_other = other_core(routed)
    x_other = other_core(x_mine)
    up_w, down_w, cut = fetch(expert_up[0], expert_down[0], projection_t, routed)
    projection_other = other_core(cut)
    keep, send = experts(
        routed, routed_other, teacher_gain[None, :], expert_gate[0], up_w, down_w
    )
    outputs = merge(keep, other_core(send), projection_other)
    s_keep, s_send, act, pre, factor, x_all = forward(
        x_mine,
        x_other,
        student_gate.T,
        student_up.T,
        student_down,
        gain_row,
        outputs,
    )
    returned = exchange(outputs)
    joint = combine(returned, teacher_in, routes, gates, s_keep, other_core(s_send))
    near, far = targets(exchange(joint), projection_t, projection_other, student_t)
    d_mine = exchange(deltas(near, other_core(far), chips))
    d_other = other_core(d_mine)
    grad_gate, grad_up, grad_down, mse = backward(
        d_mine, d_other, x_all, student_down, act, pre, factor, gain_row
    )
    return (grad_gate.T, grad_up.T, grad_down, mse.reshape(()))


def solution(mesh):
    everything = ("grp", "ep", "rep")
    placed = (
        P("ep", None),
        P(),
        P("ep", None),
        P("ep", None),
        P("ep", None, ("grp", "rep")),
        P("ep", None, ("grp", "rep")),
        P("ep", ("grp", "rep"), None),
        P(None, everything),
        P(None, everything),
        P(),
        P(None, everything),
        P(None, everything),
        P(everything, None),
    )
    return jax.shard_map(
        local,
        mesh=mesh,
        in_specs=placed,
        out_specs=(P(None, everything), P(None, everything), P(everything, None), P()),
        check_vma=False,
    )
```

```python
import math

import jax
import jax.numpy as jnp
from jax import lax
from jax.experimental import pallas as pl
from jax.experimental.pallas import tpu as pltpu
from jax.sharding import PartitionSpec as P

CHIPS = ("grp", "ep")
NN = (((1,), (0,)), ((), ()))
NT = (((1,), (1,)), ((), ()))
TN = (((0,), (0,)), ((), ()))
LANES = 128


def dot(a, b, dims=NN):
    return lax.dot_general(a, b, dims, preferred_element_type=jnp.float32)


def silu(v):
    return v / (1.0 + jnp.exp(-v))


def params(mebibytes):
    return pltpu.CompilerParams(vmem_limit_bytes=mebibytes * 1024 * 1024)


def cost(microseconds):
    flops = int(microseconds * 1e9)
    return pl.CostEstimate(flops=flops, bytes_accessed=0, transcendentals=0)


def vmem():
    return pl.BlockSpec(memory_space=pltpu.VMEM)


def anywhere():
    return pl.BlockSpec(memory_space=pl.ANY)


def in_hbm():
    return pl.BlockSpec(memory_space=pltpu.HBM)


def exchange(blocks):
    return lax.all_to_all(blocks, CHIPS, split_axis=0, concat_axis=0, tiled=True)


def other_core(values):
    return lax.ppermute(values, "rep", [(0, 1), (1, 0)])


def slot_weights(routes, gates, experts, copies):
    tokens, _ = routes.shape
    row = lax.broadcasted_iota(jnp.int32, (copies * experts * 2, routes.shape[1]), 0)
    expert, slot = (row // 2) % experts, (row % 2)[:, :1]
    earlier = jnp.zeros(slot.shape, jnp.float32)
    weights = []
    for t in range(tokens):
        hits = routes[t : t + 1, :] == expert
        taken = jnp.sum(jnp.where(hits, 1.0, 0.0), axis=1, keepdims=True)
        value = jnp.sum(jnp.where(hits, gates[t : t + 1, :], 0.0), axis=1, keepdims=True)
        weights.append(jnp.where(earlier == slot.astype(jnp.float32), value, 0.0))
        earlier += taken
    return weights


def padded_pieces(pieces):
    return -(-pieces // 8) * 8


def dispatch_kernel(tokens_hbm, routes_hbm, student_hbm, out, rows, tokens, routes, student, sems):
    pairs = ((routes_hbm, routes), (tokens_hbm, tokens), (student_hbm, student))
    copies_in = [pltpu.make_async_copy(a, b, sems.at[n]) for n, (a, b) in enumerate(pairs)]
    for copy in copies_in:
        copy.start()
    for copy in copies_in:
        copy.wait()
    copies = lax.axis_size("grp")
    experts = lax.axis_size("ep")
    quarter = tokens.shape[1] // (copies * lax.axis_size("rep"))
    place = lax.axis_index("rep") * copies + lax.axis_index("grp")
    start = pl.multiple_of(place * quarter, quarter)
    ids = routes[...]
    chosen = slot_weights(ids, jnp.ones(ids.shape, jnp.float32), experts, 1)
    pieces = quarter // LANES
    stride = padded_pieces(pieces)
    rows[...] = jnp.zeros(rows.shape, jnp.float32)
    for n in range(pieces):
        values = tokens[:, pl.ds(start + n * LANES, LANES)].astype(jnp.float32)
        picked = sum(c * values[t : t + 1, :] for t, c in enumerate(chosen))
        rows[pl.ds(n, 2 * experts, stride=stride), :] = picked
    here = student.shape[0]
    routed = rows[...].astype(jnp.bfloat16).reshape(experts, 2 * stride, LANES)
    for n in range(copies):
        out[n * experts : (n + 1) * experts, here:, :] = routed
    block = student[...]
    out[:, :here, :] = jnp.broadcast_to(block[None], (out.shape[0],) + block.shape)


def dispatch(tokens, routes, student):
    copies, experts = lax.axis_size("grp"), lax.axis_size("ep")
    rows = 2 * padded_pieces(tokens.shape[1] // (copies * lax.axis_size("rep") * LANES))
    shape = (copies * experts, student.shape[0] + rows, LANES)
    return pl.pallas_call(
        dispatch_kernel,
        out_shape=jax.ShapeDtypeStruct(shape, jnp.bfloat16),
        in_specs=[in_hbm()] * 3,
        out_specs=vmem(),
        scratch_shapes=[
            pltpu.VMEM((experts * rows, LANES), jnp.float32),
            pltpu.VMEM(tokens.shape, tokens.dtype),
            pltpu.VMEM(routes.shape, routes.dtype),
            pltpu.VMEM(student.shape, student.dtype),
            pltpu.SemaphoreType.DMA((3,)),
        ],
        compiler_params=params(8),
        cost_estimate=cost(30),
        name="dispatch",
    )(*[pltpu.with_memory_space_constraint(a, pltpu.HBM) for a in (tokens, routes, student)])


def scaled_tokens(source, gains, rows, scaled):
    routed = rows.shape[0]
    groups = lax.axis_size("grp")
    slots, half = scaled.shape
    pieces = half // (groups * LANES)
    stride = padded_pieces(pieces)
    rows[...] = source.astype(jnp.float32).reshape(routed, LANES)
    squares = jnp.zeros((slots, LANES), jnp.float32)
    for g in range(groups):
        for m in range(pieces):
            column = (g * pieces + m) * LANES
            columns = slice(column, column + LANES)
            values = rows[pl.ds(g * slots * stride + m, slots, stride=stride), :]
            squares += values * values
            scaled[:, columns] = (values * gains[:, columns]).astype(jnp.bfloat16)
    return squares


def first_half_kernel(
    routed, gain, gate_w, up_w, projection, pre, squares, cut, rows, scaled, sem
):
    half = scaled.shape[1]
    core = lax.axis_index("rep")
    start = pl.multiple_of(core * half, half)
    cut_start = pl.multiple_of((1 - core) * half, half)
    copy = pltpu.make_async_copy(projection.at[:, pl.ds(cut_start, half)], cut, sem)
    copy.start()
    gains = gain[:, pl.ds(start, half)]
    squares[...] = scaled_tokens(routed[...], gains, rows, scaled)
    values = scaled[...]
    pre[0] = dot(values, gate_w[pl.ds(start, half), :])
    pre[1] = dot(values, up_w[pl.ds(start, half), :])
    copy.wait()


def first_half(routed, gain, gate, up, projection):
    slots = 2 * lax.axis_size("ep")
    half = gain.shape[1] // 2
    return pl.pallas_call(
        first_half_kernel,
        out_shape=(
            jax.ShapeDtypeStruct((2, slots, gate.shape[1]), jnp.float32),
            jax.ShapeDtypeStruct((slots, LANES), jnp.float32),
            jax.ShapeDtypeStruct((projection.shape[0], half), projection.dtype),
        ),
        in_specs=[vmem()] * 4 + [in_hbm()],
        out_specs=(vmem(),) * 3,
        scratch_shapes=[
            pltpu.VMEM((routed.shape[0] * routed.shape[1], LANES), jnp.float32),
            pltpu.VMEM((slots, half), jnp.bfloat16),
            pltpu.SemaphoreType.DMA,
        ],
        compiler_params=params(8),
        cost_estimate=cost(2),
        name="first_half",
    )(routed, gain, gate, up, pltpu.with_memory_space_constraint(projection, pltpu.HBM))


def expert_kernel(
    other, pre, squares, gain, gate_w, up_w, down_w, keep, send, token, rows, scaled, result
):
    slots, half = scaled.shape
    pieces = half // (lax.axis_size("grp") * LANES)
    stride = padded_pieces(pieces)
    core = lax.axis_index("rep")
    first = pl.multiple_of(core * half, half)
    second = pl.multiple_of((1 - core) * half, half)
    total = squares[...]
    total += scaled_tokens(other[...], gain[:, pl.ds(second, half)], rows, scaled)
    factor = lax.rsqrt(jnp.sum(total, axis=1, keepdims=True) / (2 * half) + 1e-05)
    token[...] = jnp.zeros(token.shape, token.dtype)
    values = scaled[...]
    gate_pre = (pre[0] + dot(values, gate_w[pl.ds(second, half), :])) * factor
    up_pre = (pre[1] + dot(values, up_w[pl.ds(second, half), :])) * factor
    hidden = (silu(gate_pre) * up_pre).astype(jnp.bfloat16)
    width = half // 2
    result[...] = jnp.zeros(result.shape, jnp.float32)
    for dst, start in ((send, second), (keep, first)):
        for n in range(2):
            columns = pl.ds(pl.multiple_of(start + n * width, width), width)
            out = dot(hidden, down_w[:, columns])
            for m in range(pieces):
                place = pl.ds(n * slots * stride + m, slots, stride=stride)
                result[place, :] = out[:, m * LANES : (m + 1) * LANES]
        dst[...] = result[...].astype(dst.dtype)


def experts(other, pre, squares, gain, w_gate, w_up, w_down):
    groups, slots = lax.axis_size("grp"), squares.shape[0]
    half = gain.shape[1] // 2
    result = (groups * slots * padded_pieces(half // (groups * LANES)), LANES)
    return pl.pallas_call(
        expert_kernel,
        out_shape=(
            jax.ShapeDtypeStruct(result, jnp.float32),
            jax.ShapeDtypeStruct(result, jnp.bfloat16),
            jax.ShapeDtypeStruct((8, LANES), jnp.float32),
        ),
        in_specs=[vmem()] * 7,
        out_specs=(vmem(),) * 3,
        scratch_shapes=[
            pltpu.VMEM(result, jnp.float32),
            pltpu.VMEM((slots, half), jnp.bfloat16),
            pltpu.VMEM(result, jnp.float32),
        ],
        compiler_params=params(8),
        cost_estimate=cost(3),
        name="experts",
    )(other, pre, squares, gain, w_gate, w_up, w_down)


def combine_kernel(returned, tokens, routes, gates, keep, received, out, rows, own):
    copies = lax.axis_size("grp")
    experts = lax.axis_size("ep")
    slots = 2 * copies * experts
    stride = returned.shape[0] // slots
    quarter = tokens.shape[1] // (copies * lax.axis_size("rep"))
    pieces = quarter // LANES
    place = lax.axis_index("rep") * copies + lax.axis_index("grp")
    start = pl.multiple_of(place * quarter, quarter)
    count = tokens.shape[0]
    weights = slot_weights(routes[...], gates[...], experts, copies)
    weights = [jnp.broadcast_to(w, (slots, LANES)) for w in weights]
    rows[...] = returned[...].astype(jnp.float32)
    for m in range(pieces):
        values = rows[pl.ds(m, slots, stride=stride), :]
        before = tokens[:, pl.ds(start + m * LANES, LANES)].astype(jnp.float32)
        for t in range(count):
            moe = jnp.sum(values * weights[t], axis=0, keepdims=True)
            own[t * pieces + m : t * pieces + m + 1, :] = before[t : t + 1, :] + moe
    here = keep.shape[1]
    block = own[...].astype(jnp.bfloat16)
    out[:, :here, :] = (keep[...] + received[...].astype(jnp.float32)).astype(jnp.bfloat16)
    out[:, here:, :] = jnp.broadcast_to(block[None], (out.shape[0],) + block.shape)


def combine(returned, tokens, routes, gates, keep, received):
    chips, rows, _ = keep.shape
    own = tokens.size // (lax.axis_size("grp") * lax.axis_size("rep") * LANES)
    return pl.pallas_call(
        combine_kernel,
        out_shape=jax.ShapeDtypeStruct((chips, rows + own, LANES), jnp.bfloat16),
        in_specs=[vmem()] * 6,
        out_specs=vmem(),
        scratch_shapes=[
            pltpu.VMEM(returned.shape, jnp.float32),
            pltpu.VMEM((own, LANES), jnp.float32),
        ],
        compiler_params=params(16),
        cost_estimate=cost(4),
        name="combine",
    )(returned, tokens, routes, gates, keep, received)


def split_kernel(arrived, *refs):
    routed = refs[-1]
    routed[...] = arrived[:, arrived.shape[1] - routed.shape[1] :, :]


def split(arrived, rows, weights):
    chips, total, lanes = arrived.shape
    return pl.pallas_call(
        split_kernel,
        out_shape=jax.ShapeDtypeStruct((chips, total - rows, lanes), arrived.dtype),
        in_specs=[vmem()] * (1 + len(weights)),
        out_specs=vmem(),
        compiler_params=params(4),
        cost_estimate=cost(1),
        name="split",
    )(arrived, *weights)


def split_student_kernel(arrived, other, squares, student):
    del other, squares
    student[...] = arrived[:, : student.shape[1], :]


def split_student(arrived, rows, *after):
    chips, _, lanes = arrived.shape
    return pl.pallas_call(
        split_student_kernel,
        out_shape=jax.ShapeDtypeStruct((chips, rows, lanes), arrived.dtype),
        in_specs=[vmem()] + [anywhere()] * 2,
        out_specs=vmem(),
        compiler_params=params(4),
        cost_estimate=cost(1),
        name="split_student",
    )(arrived, *after)


def merge_kernel(keep, received, after, out):
    out[...] = (keep[...] + received[...].astype(jnp.float32)).astype(out.dtype)


def merge(keep, received, after):
    return pl.pallas_call(
        merge_kernel,
        out_shape=jax.ShapeDtypeStruct(received.shape, received.dtype),
        in_specs=[vmem()] * 2 + [anywhere()],
        out_specs=vmem(),
        compiler_params=params(6),
        cost_estimate=cost(1),
        name="merge",
    )(keep, received, after)


def start_interleaved(mine, other, dst, sems):
    core = lax.axis_index("rep")
    copies = [
        pltpu.make_async_copy(mine, dst.at[:, core], sems.at[0]),
        pltpu.make_async_copy(other, dst.at[:, 1 - core], sems.at[1]),
    ]
    for copy in copies:
        copy.start()
    return copies


def forward_kernel(mine, other, gate, up, down, gain, after, keep, *refs):
    send, act_ref, pre_ref, factor_ref, x, scaled, sems = refs
    core = lax.axis_index("rep")
    chips, cores, rows, tokens = x.shape
    features = chips * cores * rows
    hidden = down.shape[0]
    copies = start_interleaved(mine, other, x, sems)
    for n, weights in enumerate((gate, up)):
        part = (weights[...].astype(jnp.float32) * gain[...]).astype(jnp.bfloat16)
        scaled[n * hidden : (n + 1) * hidden, :] = part
    for copy in copies:
        copy.wait()
    values = x[...].reshape(features, tokens)
    floats = values.astype(jnp.float32)
    factor = lax.rsqrt(jnp.sum(floats * floats, axis=0, keepdims=True) / features + 1e-05)
    factor_ref[...] = factor
    pre = dot(scaled[...], values) * factor
    pre_ref[...] = pre
    act = (silu(pre[:hidden]) * pre[hidden:]).astype(jnp.bfloat16)
    act_ref[...] = act
    step = 8
    width = step * 2 * rows
    for n in range(chips // step):
        part = dot(down[:, n * width : (n + 1) * width], act, TN).reshape(step, 2, rows, tokens)
        here = slice(n * step, (n + 1) * step)
        low, high = part[:, 0], part[:, 1]
        keep[here] = jnp.where(core == 0, low, high)
        send[here] = jnp.where(core == 0, high, low).astype(jnp.bfloat16)


def forward(mine, other, gate, up, down, gain, after):
    chips, _, tokens = mine.shape
    hidden, features = down.shape
    rows = features // (2 * chips)
    whole = (chips, 2, rows, tokens)
    return pl.pallas_call(
        forward_kernel,
        out_shape=(
            jax.ShapeDtypeStruct((chips, rows, tokens), jnp.float32),
            jax.ShapeDtypeStruct((chips, rows, tokens), jnp.bfloat16),
            jax.ShapeDtypeStruct((hidden, tokens), jnp.bfloat16),
            jax.ShapeDtypeStruct((2 * hidden, tokens), jnp.float32),
            jax.ShapeDtypeStruct((1, tokens), jnp.float32),
            jax.ShapeDtypeStruct(whole, jnp.bfloat16),
        ),
        in_specs=[anywhere()] * 2 + [vmem()] * 4 + [anywhere()],
        out_specs=(vmem(),) * 6,
        scratch_shapes=[
            pltpu.VMEM((2 * hidden, features), jnp.bfloat16),
            pltpu.SemaphoreType.DMA((2,)),
        ],
        compiler_params=params(20),
        cost_estimate=cost(8),
        name="forward",
    )(mine, other, gate, up, down, gain, after)


def target_kernel(arrived, projection, projection_other, student_in, near, far, rows, tokens):
    here = student_in.shape[0]
    chips, total, lanes = arrived.shape
    count, half = tokens.shape
    groups = lax.axis_size("grp")
    pieces = half // (groups * lanes)
    start = pl.multiple_of(lax.axis_index("rep") * half, half)
    rows[...] = arrived[:, here:, :].astype(jnp.float32).reshape(rows.shape)
    for g in range(groups):
        for m in range(pieces):
            place = pl.ds(g * count * pieces + m, count, stride=pieces)
            columns = slice((g * pieces + m) * lanes, (g * pieces + m + 1) * lanes)
            tokens[:, columns] = rows[place, :].astype(jnp.bfloat16)
    values = tokens[...]
    far[...] = dot(projection_other[...], values, NT)
    branch = jnp.sum(arrived[:, :here, :].astype(jnp.float32), axis=0)
    target = dot(projection[:, pl.ds(start, half)], values, NT)
    near[...] = student_in[...].astype(jnp.float32) + branch - target


def targets(arrived, projection, projection_other, student_in):
    here, count = student_in.shape
    chips, total, lanes = arrived.shape
    half = projection_other.shape[1]
    part = jax.ShapeDtypeStruct((here, count), jnp.float32)
    return pl.pallas_call(
        target_kernel,
        out_shape=(part, part),
        in_specs=[vmem()] * 4,
        out_specs=(vmem(),) * 2,
        scratch_shapes=[
            pltpu.VMEM((chips * (total - here), lanes), jnp.float32),
            pltpu.VMEM((count, half), jnp.bfloat16),
        ],
        compiler_params=params(16),
        cost_estimate=cost(4),
        name="targets",
    )(arrived, projection, projection_other, student_in)


def delta_kernel(near, far, delta):
    tokens = near.shape[1]
    scaled = ((near[...] - far[...]) / math.sqrt(tokens)).astype(jnp.bfloat16)
    delta[...] = jnp.broadcast_to(scaled[None], delta.shape)


def deltas(near, far, chips):
    return pl.pallas_call(
        delta_kernel,
        out_shape=jax.ShapeDtypeStruct((chips,) + near.shape, jnp.bfloat16),
        in_specs=[vmem()] * 2,
        out_specs=vmem(),
        compiler_params=params(4),
        cost_estimate=cost(1),
        name="deltas",
    )(near, far)


def backward_kernel(
    d_mine,
    d_other,
    x,
    down,
    act,
    pre,
    factor,
    gain,
    grad_gate_hbm,
    grad_up_hbm,
    grad_down_hbm,
    mse,
    d,
    grad_gate,
    grad_up,
    grad_down,
    sems_d,
    sems_out,
):
    chips, _, rows, tokens = d.shape
    features = chips * 2 * rows
    copies_d = start_interleaved(d_mine, d_other, d, sems_d)
    for copy in copies_d:
        copy.wait()
    hidden = act.shape[0]
    step = 8
    width = step * 2 * rows
    acts = act[...]
    copies = []

    def send_out(kind, n, src, dst):
        here = slice(n * width, (n + 1) * width)
        copy = pltpu.make_async_copy(src.at[:, here], dst.at[:, here], sems_out.at[kind, n])
        copy.start()
        copies.append(copy)

    total = jnp.zeros((1, tokens), jnp.float32)
    for n in range(chips // step):
        here = slice(n * width, (n + 1) * width)
        part = d[n * step : (n + 1) * step].reshape(width, tokens)
        grad_down[:, here] = dot(acts, part, NT).astype(jnp.bfloat16)
        send_out(0, n, grad_down, grad_down_hbm)
        floats = part.astype(jnp.float32)
        total += jnp.sum(floats * floats, axis=0, keepdims=True)
    mse[...] = jnp.sum(total, axis=1, keepdims=True) / features
    delta = d[...].reshape(features, tokens)
    back = dot(down[...], delta)
    gate_pre, up_pre = pre[:hidden], pre[hidden:]
    sigmoid = 1.0 / (1.0 + jnp.exp(-gate_pre))
    d_gate = back * up_pre * sigmoid * (1.0 + gate_pre * (1.0 - sigmoid))
    d_up = back * gate_pre * sigmoid
    scale = factor[...]
    d_both = jnp.concatenate([d_gate * scale, d_up * scale], axis=0).astype(jnp.bfloat16)
    for n in range(chips // step):
        here = slice(n * width, (n + 1) * width)
        part = x[n * step : (n + 1) * step].reshape(width, tokens)
        grads = dot(d_both, part, NT) * gain[:, here]
        grad_gate[:, here] = grads[:hidden].astype(jnp.bfloat16)
        grad_up[:, here] = grads[hidden:].astype(jnp.bfloat16)
        send_out(1, n, grad_gate, grad_gate_hbm)
        send_out(2, n, grad_up, grad_up_hbm)
    for copy in copies:
        copy.wait()


def backward(d_mine, d_other, x, down, act, pre, factor, gain):
    chips, rows, tokens = d_mine.shape
    hidden, features = down.shape
    grad = jax.ShapeDtypeStruct((hidden, features), jnp.bfloat16)
    whole = pltpu.VMEM((chips, 2, rows, tokens), jnp.bfloat16)
    return pl.pallas_call(
        backward_kernel,
        out_shape=(grad, grad, grad, jax.ShapeDtypeStruct((1, 1), jnp.float32)),
        in_specs=[anywhere()] * 2 + [vmem()] * 6,
        out_specs=(anywhere(),) * 3 + (vmem(),),
        scratch_shapes=[
            whole,
            *[pltpu.VMEM((hidden, features), jnp.bfloat16)] * 3,
            pltpu.SemaphoreType.DMA((2,)),
            pltpu.SemaphoreType.DMA((3, 8)),
        ],
        compiler_params=params(24),
        cost_estimate=cost(8),
        name="backward",
    )(d_mine, d_other, x, down, act, pre, factor, gain)


def local(
    teacher_in,
    teacher_gain,
    routes,
    gates,
    expert_gate,
    expert_up,
    expert_down,
    projection,
    student_in,
    student_gain,
    student_gate,
    student_up,
    student_down,
):
    chips = lax.axis_size(CHIPS)
    projection_t = projection.T
    student_t = student_in.T
    gain_row = student_gain[None, :]

    arrived = exchange(dispatch(teacher_in, routes, student_t))
    expert_weights = (expert_gate[0], expert_up[0], expert_down[0])
    student_weights = (student_gate.T, student_up.T, student_down)
    here = student_t.shape[0]
    routed = split(arrived, here, expert_weights + student_weights)
    routed_other = other_core(routed)
    teacher_row = teacher_gain[None, :]
    first_pre, squares, cut = first_half(routed, teacher_row, *expert_weights[:2], projection_t)
    x_mine = split_student(arrived, here, routed_other, squares)
    x_other = other_core(x_mine)
    projection_other = other_core(cut)
    keep, send, token = experts(routed_other, first_pre, squares, teacher_row, *expert_weights)
    s_keep, s_send, act, pre, factor, x_all = forward(
        x_mine, x_other, *student_weights, gain_row, token
    )
    outputs = merge(keep, other_core(send), projection_other)
    returned = exchange(outputs)
    joint = combine(returned, teacher_in, routes, gates, s_keep, other_core(s_send))
    near, far = targets(exchange(joint), projection_t, projection_other, student_t)
    d_mine = exchange(deltas(near, other_core(far), chips))
    d_other = other_core(d_mine)
    grad_gate, grad_up, grad_down, mse = backward(
        d_mine, d_other, x_all, student_down, act, pre, factor, gain_row
    )
    return (grad_gate.T, grad_up.T, grad_down, mse.reshape(()))


def solution(mesh):
    everything = ("grp", "ep", "rep")
    placed = (
        P("ep", None),
        P(),
        P("ep", None),
        P("ep", None),
        P("ep", None, ("grp", "rep")),
        P("ep", None, ("grp", "rep")),
        P("ep", ("grp", "rep"), None),
        P(None, everything),
        P(None, everything),
        P(),
        P(None, everything),
        P(None, everything),
        P(everything, None),
    )
    return jax.shard_map(
        local,
        mesh=mesh,
        in_specs=placed,
        out_specs=(P(None, everything), P(None, everything), P(everything, None), P()),
        check_vma=False,
    )
```

```python
import math

import jax
import jax.numpy as jnp
from jax import lax
from jax.experimental import pallas as pl
from jax.experimental.pallas import tpu as pltpu
from jax.sharding import PartitionSpec as P

CHIPS = ("grp", "ep")
NN = (((1,), (0,)), ((), ()))
NT = (((1,), (1,)), ((), ()))
TN = (((0,), (0,)), ((), ()))
LANES = 128


def dot(a, b, dims=NN):
    return lax.dot_general(a, b, dims, preferred_element_type=jnp.float32)


def silu(v):
    return v / (1.0 + jnp.exp(-v))


def params(mebibytes):
    return pltpu.CompilerParams(vmem_limit_bytes=mebibytes * 1024 * 1024)


def cost(microseconds):
    flops = int(microseconds * 1e9)
    return pl.CostEstimate(flops=flops, bytes_accessed=0, transcendentals=0)


def vmem():
    return pl.BlockSpec(memory_space=pltpu.VMEM)


def anywhere():
    return pl.BlockSpec(memory_space=pl.ANY)


def in_hbm():
    return pl.BlockSpec(memory_space=pltpu.HBM)


def exchange(blocks):
    return lax.all_to_all(blocks, CHIPS, split_axis=0, concat_axis=0, tiled=True)


def other_core(values):
    return lax.ppermute(values, "rep", [(0, 1), (1, 0)])


def slot_weights(routes, gates, experts, copies):
    tokens, _ = routes.shape
    row = lax.broadcasted_iota(jnp.int32, (copies * experts * 2, routes.shape[1]), 0)
    expert, slot = (row // 2) % experts, (row % 2)[:, :1]
    earlier = jnp.zeros(slot.shape, jnp.float32)
    weights = []
    for t in range(tokens):
        hits = routes[t : t + 1, :] == expert
        taken = jnp.sum(jnp.where(hits, 1.0, 0.0), axis=1, keepdims=True)
        value = jnp.sum(jnp.where(hits, gates[t : t + 1, :], 0.0), axis=1, keepdims=True)
        weights.append(jnp.where(earlier == slot.astype(jnp.float32), value, 0.0))
        earlier += taken
    return weights


def padded_pieces(pieces):
    return -(-pieces // 8) * 8


def dispatch_kernel(
    tokens_hbm,
    routes_hbm,
    student_hbm,
    gain_hbm,
    out,
    rows,
    tokens,
    routes,
    student,
    gain,
    sems,
):
    chip = lax.axis_index("grp") * lax.axis_size("ep") + lax.axis_index("ep")
    mine = pl.ds(pl.multiple_of(chip * LANES, LANES), LANES)
    pairs = (
        (routes_hbm, routes),
        (tokens_hbm, tokens),
        (student_hbm, student),
        (gain_hbm.at[:, mine], gain),
    )
    copies_in = [pltpu.make_async_copy(a, b, sems.at[n]) for n, (a, b) in enumerate(pairs)]
    for copy in copies_in:
        copy.start()
    for copy in copies_in:
        copy.wait()
    copies = lax.axis_size("grp")
    experts = lax.axis_size("ep")
    quarter = tokens.shape[1] // (copies * lax.axis_size("rep"))
    place = lax.axis_index("rep") * copies + lax.axis_index("grp")
    start = pl.multiple_of(place * quarter, quarter)
    ids = routes[...]
    chosen = slot_weights(ids, jnp.ones(ids.shape, jnp.float32), experts, 1)
    pieces = quarter // LANES
    stride = padded_pieces(pieces)
    rows[...] = jnp.zeros(rows.shape, jnp.float32)
    for n in range(pieces):
        values = tokens[:, pl.ds(start + n * LANES, LANES)].astype(jnp.float32)
        picked = sum(c * values[t : t + 1, :] for t, c in enumerate(chosen))
        rows[pl.ds(n, 2 * experts, stride=stride), :] = picked
    here = student.shape[0]
    values = student[...].astype(jnp.float32)
    squares = jnp.sum(values * values, axis=0, keepdims=True)
    high = squares.astype(jnp.bfloat16).astype(jnp.float32)
    for n, part in enumerate((high, squares - high)):
        place = pl.ds(pieces + n, 2 * experts, stride=stride)
        rows[place, :] = jnp.broadcast_to(part, (2 * experts, LANES))
    routed = rows[...].astype(jnp.bfloat16).reshape(experts, 2 * stride, LANES)
    for n in range(copies):
        out[n * experts : (n + 1) * experts, here:, :] = routed
    columns = jnp.broadcast_to(gain[...], (LANES, LANES)).T
    columns = jnp.where(lax.axis_index("rep") == 0, columns[:here], columns[here:])
    block = (values * columns).astype(jnp.bfloat16)
    out[:, :here, :] = jnp.broadcast_to(block[None], (out.shape[0],) + block.shape)


def dispatch(tokens, routes, student, gain):
    copies, experts = lax.axis_size("grp"), lax.axis_size("ep")
    rows = 2 * padded_pieces(tokens.shape[1] // (copies * lax.axis_size("rep") * LANES))
    shape = (copies * experts, student.shape[0] + rows, LANES)
    return pl.pallas_call(
        dispatch_kernel,
        out_shape=jax.ShapeDtypeStruct(shape, jnp.bfloat16),
        in_specs=[in_hbm()] * 4,
        out_specs=vmem(),
        scratch_shapes=[
            pltpu.VMEM((experts * rows, LANES), jnp.float32),
            pltpu.VMEM(tokens.shape, tokens.dtype),
            pltpu.VMEM(routes.shape, routes.dtype),
            pltpu.VMEM(student.shape, student.dtype),
            pltpu.VMEM((1, LANES), gain.dtype),
            pltpu.SemaphoreType.DMA((4,)),
        ],
        compiler_params=params(8),
        cost_estimate=cost(30),
        name="dispatch",
    )(
        *[
            pltpu.with_memory_space_constraint(a, pltpu.HBM)
            for a in (tokens, routes, student, gain)
        ]
    )


def scaled_tokens(source, gains, rows, scaled):
    routed = rows.shape[0]
    groups = lax.axis_size("grp")
    slots, half = scaled.shape
    pieces = half // (groups * LANES)
    stride = padded_pieces(pieces)
    rows[...] = source.astype(jnp.float32).reshape(routed, LANES)
    squares = jnp.zeros((slots, LANES), jnp.float32)
    for g in range(groups):
        for m in range(pieces):
            column = (g * pieces + m) * LANES
            columns = slice(column, column + LANES)
            values = rows[pl.ds(g * slots * stride + m, slots, stride=stride), :]
            squares += values * values
            scaled[:, columns] = (values * gains[:, columns]).astype(jnp.bfloat16)
    return squares


def first_half_kernel(
    routed, gain, gate_w, up_w, projection, pre, squares, cut, rows, scaled, sem
):
    half = scaled.shape[1]
    core = lax.axis_index("rep")
    start = pl.multiple_of(core * half, half)
    cut_start = pl.multiple_of((1 - core) * half, half)
    copy = pltpu.make_async_copy(projection.at[:, pl.ds(cut_start, half)], cut, sem)
    copy.start()
    gains = gain[:, pl.ds(start, half)]
    squares[...] = scaled_tokens(routed[...], gains, rows, scaled)
    values = scaled[...]
    pre[0] = dot(values, gate_w[pl.ds(start, half), :])
    pre[1] = dot(values, up_w[pl.ds(start, half), :])
    copy.wait()


def first_half(routed, gain, gate, up, projection):
    slots = 2 * lax.axis_size("ep")
    half = gain.shape[1] // 2
    return pl.pallas_call(
        first_half_kernel,
        out_shape=(
            jax.ShapeDtypeStruct((2, slots, gate.shape[1]), jnp.float32),
            jax.ShapeDtypeStruct((slots, LANES), jnp.float32),
            jax.ShapeDtypeStruct((projection.shape[0], half), projection.dtype),
        ),
        in_specs=[vmem()] * 4 + [in_hbm()],
        out_specs=(vmem(),) * 3,
        scratch_shapes=[
            pltpu.VMEM((routed.shape[0] * routed.shape[1], LANES), jnp.float32),
            pltpu.VMEM((slots, half), jnp.bfloat16),
            pltpu.SemaphoreType.DMA,
        ],
        compiler_params=params(8),
        cost_estimate=cost(2),
        name="first_half",
    )(routed, gain, gate, up, pltpu.with_memory_space_constraint(projection, pltpu.HBM))


def expert_kernel(
    other, pre, squares, gain, gate_w, up_w, down_w, keep, send, token, rows, scaled, result
):
    slots, half = scaled.shape
    pieces = half // (lax.axis_size("grp") * LANES)
    stride = padded_pieces(pieces)
    core = lax.axis_index("rep")
    first = pl.multiple_of(core * half, half)
    second = pl.multiple_of((1 - core) * half, half)
    total = squares[...]
    total += scaled_tokens(other[...], gain[:, pl.ds(second, half)], rows, scaled)
    factor = lax.rsqrt(jnp.sum(total, axis=1, keepdims=True) / (2 * half) + 1e-05)
    token[...] = jnp.zeros(token.shape, token.dtype)
    values = scaled[...]
    gate_pre = (pre[0] + dot(values, gate_w[pl.ds(second, half), :])) * factor
    up_pre = (pre[1] + dot(values, up_w[pl.ds(second, half), :])) * factor
    hidden = (silu(gate_pre) * up_pre).astype(jnp.bfloat16)
    width = half // 2
    result[...] = jnp.zeros(result.shape, jnp.float32)
    for dst, start in ((send, second), (keep, first)):
        for n in range(2):
            columns = pl.ds(pl.multiple_of(start + n * width, width), width)
            out = dot(hidden, down_w[:, columns])
            for m in range(pieces):
                place = pl.ds(n * slots * stride + m, slots, stride=stride)
                result[place, :] = out[:, m * LANES : (m + 1) * LANES]
        dst[...] = result[...].astype(dst.dtype)


def experts(other, pre, squares, gain, w_gate, w_up, w_down):
    groups, slots = lax.axis_size("grp"), squares.shape[0]
    half = gain.shape[1] // 2
    result = (groups * slots * padded_pieces(half // (groups * LANES)), LANES)
    return pl.pallas_call(
        expert_kernel,
        out_shape=(
            jax.ShapeDtypeStruct(result, jnp.float32),
            jax.ShapeDtypeStruct(result, jnp.bfloat16),
            jax.ShapeDtypeStruct((8, LANES), jnp.float32),
        ),
        in_specs=[vmem()] * 7,
        out_specs=(vmem(),) * 3,
        scratch_shapes=[
            pltpu.VMEM(result, jnp.float32),
            pltpu.VMEM((slots, half), jnp.bfloat16),
            pltpu.VMEM(result, jnp.float32),
        ],
        compiler_params=params(8),
        cost_estimate=cost(3),
        name="experts",
    )(other, pre, squares, gain, w_gate, w_up, w_down)


def combine_kernel(returned, tokens, routes, gates, keep, received, out, rows, own):
    copies = lax.axis_size("grp")
    experts = lax.axis_size("ep")
    slots = 2 * copies * experts
    stride = returned.shape[0] // slots
    quarter = tokens.shape[1] // (copies * lax.axis_size("rep"))
    pieces = quarter // LANES
    place = lax.axis_index("rep") * copies + lax.axis_index("grp")
    start = pl.multiple_of(place * quarter, quarter)
    count = tokens.shape[0]
    weights = slot_weights(routes[...], gates[...], experts, copies)
    weights = [jnp.broadcast_to(w, (slots, LANES)) for w in weights]
    rows[...] = returned[...].astype(jnp.float32)
    for m in range(pieces):
        values = rows[pl.ds(m, slots, stride=stride), :]
        before = tokens[:, pl.ds(start + m * LANES, LANES)].astype(jnp.float32)
        for t in range(count):
            moe = jnp.sum(values * weights[t], axis=0, keepdims=True)
            own[t * pieces + m : t * pieces + m + 1, :] = before[t : t + 1, :] + moe
    here = keep.shape[1]
    block = own[...].astype(jnp.bfloat16)
    out[:, :here, :] = (keep[...] + received[...].astype(jnp.float32)).astype(jnp.bfloat16)
    out[:, here:, :] = jnp.broadcast_to(block[None], (out.shape[0],) + block.shape)


def combine(returned, tokens, routes, gates, keep, received):
    chips, rows, _ = keep.shape
    own = tokens.size // (lax.axis_size("grp") * lax.axis_size("rep") * LANES)
    return pl.pallas_call(
        combine_kernel,
        out_shape=jax.ShapeDtypeStruct((chips, rows + own, LANES), jnp.bfloat16),
        in_specs=[vmem()] * 6,
        out_specs=vmem(),
        scratch_shapes=[
            pltpu.VMEM(returned.shape, jnp.float32),
            pltpu.VMEM((own, LANES), jnp.float32),
        ],
        compiler_params=params(16),
        cost_estimate=cost(4),
        name="combine",
    )(returned, tokens, routes, gates, keep, received)


def split_kernel(arrived, *refs):
    routed = refs[-1]
    routed[...] = arrived[:, arrived.shape[1] - routed.shape[1] :, :]


def split(arrived, rows, weights):
    chips, total, lanes = arrived.shape
    return pl.pallas_call(
        split_kernel,
        out_shape=jax.ShapeDtypeStruct((chips, total - rows, lanes), arrived.dtype),
        in_specs=[vmem()] * (1 + len(weights)),
        out_specs=vmem(),
        compiler_params=params(4),
        cost_estimate=cost(1),
        name="split",
    )(arrived, *weights)


def split_student_kernel(arrived, other, squares, student):
    del other, squares
    student[...] = arrived[:, : student.shape[1], :]


def split_student(arrived, rows, *after):
    chips, _, lanes = arrived.shape
    return pl.pallas_call(
        split_student_kernel,
        out_shape=jax.ShapeDtypeStruct((chips, rows, lanes), arrived.dtype),
        in_specs=[vmem()] + [anywhere()] * 2,
        out_specs=vmem(),
        compiler_params=params(4),
        cost_estimate=cost(1),
        name="split_student",
    )(arrived, *after)


def merge_kernel(keep, received, after, out):
    out[...] = (keep[...] + received[...].astype(jnp.float32)).astype(out.dtype)


def merge(keep, received, after):
    return pl.pallas_call(
        merge_kernel,
        out_shape=jax.ShapeDtypeStruct(received.shape, received.dtype),
        in_specs=[vmem()] * 2 + [anywhere()],
        out_specs=vmem(),
        compiler_params=params(6),
        cost_estimate=cost(1),
        name="merge",
    )(keep, received, after)


def start_interleaved(mine, other, dst, sems):
    core = lax.axis_index("rep")
    copies = [
        pltpu.make_async_copy(mine, dst.at[:, core], sems.at[0]),
        pltpu.make_async_copy(other, dst.at[:, 1 - core], sems.at[1]),
    ]
    for copy in copies:
        copy.start()
    return copies


def forward_kernel(mine, other, routed, routed_other, gate, up, down, after, keep, *refs):
    send, act_ref, pre_ref, factor_ref, x, sems = refs
    core = lax.axis_index("rep")
    chips, cores, rows, tokens = x.shape
    features = chips * cores * rows
    hidden = down.shape[0]
    copies = start_interleaved(mine, other, x, sems)
    stride = routed.shape[1] // 2
    sums = jnp.zeros((1, tokens), jnp.float32)
    for part in (routed, routed_other):
        rows_of = part[:, stride - 2 : stride, :].astype(jnp.float32)
        sums += jnp.sum(jnp.sum(rows_of, axis=0), axis=0, keepdims=True)
    factor = lax.rsqrt(sums / features + 1e-05)
    factor_ref[...] = factor
    for copy in copies:
        copy.wait()
    values = x[...].reshape(features, tokens)
    pre_ref[:hidden, :] = dot(gate[...], values) * factor
    pre_ref[hidden:, :] = dot(up[...], values) * factor
    pre = pre_ref[...]
    act = (silu(pre[:hidden]) * pre[hidden:]).astype(jnp.bfloat16)
    act_ref[...] = act
    step = 8
    width = step * 2 * rows
    for n in range(chips // step):
        part = dot(down[:, n * width : (n + 1) * width], act, TN).reshape(step, 2, rows, tokens)
        here = slice(n * step, (n + 1) * step)
        low, high = part[:, 0], part[:, 1]
        keep[here] = jnp.where(core == 0, low, high)
        send[here] = jnp.where(core == 0, high, low).astype(jnp.bfloat16)


def forward(mine, other, routed, routed_other, gate, up, down, after):
    chips, _, tokens = mine.shape
    hidden, features = down.shape
    rows = features // (2 * chips)
    whole = (chips, 2, rows, tokens)
    return pl.pallas_call(
        forward_kernel,
        out_shape=(
            jax.ShapeDtypeStruct((chips, rows, tokens), jnp.float32),
            jax.ShapeDtypeStruct((chips, rows, tokens), jnp.bfloat16),
            jax.ShapeDtypeStruct((hidden, tokens), jnp.bfloat16),
            jax.ShapeDtypeStruct((2 * hidden, tokens), jnp.float32),
            jax.ShapeDtypeStruct((1, tokens), jnp.float32),
            jax.ShapeDtypeStruct(whole, jnp.bfloat16),
        ),
        in_specs=[anywhere()] * 2 + [vmem()] * 5 + [anywhere()],
        out_specs=(vmem(),) * 6,
        scratch_shapes=[pltpu.SemaphoreType.DMA((2,))],
        compiler_params=params(20),
        cost_estimate=cost(8),
        name="forward",
    )(mine, other, routed, routed_other, gate, up, down, after)


def target_kernel(arrived, projection, projection_other, student_in, near, far, rows, tokens):
    here = student_in.shape[0]
    chips, total, lanes = arrived.shape
    count, half = tokens.shape
    groups = lax.axis_size("grp")
    pieces = half // (groups * lanes)
    start = pl.multiple_of(lax.axis_index("rep") * half, half)
    rows[...] = arrived[:, here:, :].astype(jnp.float32).reshape(rows.shape)
    for g in range(groups):
        for m in range(pieces):
            place = pl.ds(g * count * pieces + m, count, stride=pieces)
            columns = slice((g * pieces + m) * lanes, (g * pieces + m + 1) * lanes)
            tokens[:, columns] = rows[place, :].astype(jnp.bfloat16)
    values = tokens[...]
    far[...] = dot(projection_other[...], values, NT)
    branch = jnp.sum(arrived[:, :here, :].astype(jnp.float32), axis=0)
    target = dot(projection[:, pl.ds(start, half)], values, NT)
    near[...] = student_in[...].astype(jnp.float32) + branch - target


def targets(arrived, projection, projection_other, student_in):
    here, count = student_in.shape
    chips, total, lanes = arrived.shape
    half = projection_other.shape[1]
    part = jax.ShapeDtypeStruct((here, count), jnp.float32)
    return pl.pallas_call(
        target_kernel,
        out_shape=(part, part),
        in_specs=[vmem()] * 4,
        out_specs=(vmem(),) * 2,
        scratch_shapes=[
            pltpu.VMEM((chips * (total - here), lanes), jnp.float32),
            pltpu.VMEM((count, half), jnp.bfloat16),
        ],
        compiler_params=params(16),
        cost_estimate=cost(4),
        name="targets",
    )(arrived, projection, projection_other, student_in)


def delta_kernel(near, far, delta):
    tokens = near.shape[1]
    scaled = ((near[...] - far[...]) / math.sqrt(tokens)).astype(jnp.bfloat16)
    delta[...] = jnp.broadcast_to(scaled[None], delta.shape)


def deltas(near, far, chips):
    return pl.pallas_call(
        delta_kernel,
        out_shape=jax.ShapeDtypeStruct((chips,) + near.shape, jnp.bfloat16),
        in_specs=[vmem()] * 2,
        out_specs=vmem(),
        compiler_params=params(4),
        cost_estimate=cost(1),
        name="deltas",
    )(near, far)


def backward_kernel(
    d_mine,
    d_other,
    x,
    down,
    act,
    pre,
    factor,
    grad_gate_hbm,
    grad_up_hbm,
    grad_down_hbm,
    mse,
    d,
    grad_gate,
    grad_up,
    grad_down,
    sems_d,
    sems_out,
):
    chips, _, rows, tokens = d.shape
    features = chips * 2 * rows
    copies_d = start_interleaved(d_mine, d_other, d, sems_d)
    for copy in copies_d:
        copy.wait()
    hidden = act.shape[0]
    delta = d[...].reshape(features, tokens)
    back = dot(down[...], delta)
    gate_pre, up_pre = pre[:hidden], pre[hidden:]
    sigmoid = 1.0 / (1.0 + jnp.exp(-gate_pre))
    d_gate = back * up_pre * sigmoid * (1.0 + gate_pre * (1.0 - sigmoid))
    d_up = back * gate_pre * sigmoid
    scale = factor[...]
    d_both = jnp.concatenate([d_gate * scale, d_up * scale], axis=0).astype(jnp.bfloat16)
    step = 8
    width = step * 2 * rows
    acts = act[...]
    copies = []

    def send_out(kind, n, src, dst):
        here = slice(n * width, (n + 1) * width)
        copy = pltpu.make_async_copy(src.at[:, here], dst.at[:, here], sems_out.at[kind, n])
        copy.start()
        copies.append(copy)

    total = jnp.zeros((1, tokens), jnp.float32)
    for n in range(chips // step):
        here = slice(n * width, (n + 1) * width)
        part = d[n * step : (n + 1) * step].reshape(width, tokens)
        grad_down[:, here] = dot(acts, part, NT).astype(jnp.bfloat16)
        send_out(0, n, grad_down, grad_down_hbm)
        floats = part.astype(jnp.float32)
        total += jnp.sum(floats * floats, axis=0, keepdims=True)
    mse[...] = jnp.sum(total, axis=1, keepdims=True) / features
    for n in range(chips // step):
        here = slice(n * width, (n + 1) * width)
        part = x[n * step : (n + 1) * step].reshape(width, tokens)
        grads = dot(d_both, part, NT)
        grad_gate[:, here] = grads[:hidden].astype(jnp.bfloat16)
        grad_up[:, here] = grads[hidden:].astype(jnp.bfloat16)
        send_out(1, n, grad_gate, grad_gate_hbm)
        send_out(2, n, grad_up, grad_up_hbm)
    for copy in copies:
        copy.wait()


def backward(d_mine, d_other, x, down, act, pre, factor):
    chips, rows, tokens = d_mine.shape
    hidden, features = down.shape
    grad = jax.ShapeDtypeStruct((hidden, features), jnp.bfloat16)
    whole = pltpu.VMEM((chips, 2, rows, tokens), jnp.bfloat16)
    return pl.pallas_call(
        backward_kernel,
        out_shape=(grad, grad, grad, jax.ShapeDtypeStruct((1, 1), jnp.float32)),
        in_specs=[anywhere()] * 2 + [vmem()] * 5,
        out_specs=(anywhere(),) * 3 + (vmem(),),
        scratch_shapes=[
            whole,
            *[pltpu.VMEM((hidden, features), jnp.bfloat16)] * 3,
            pltpu.SemaphoreType.DMA((2,)),
            pltpu.SemaphoreType.DMA((3, 8)),
        ],
        compiler_params=params(24),
        cost_estimate=cost(8),
        name="backward",
    )(d_mine, d_other, x, down, act, pre, factor)


def local(
    teacher_in,
    teacher_gain,
    routes,
    gates,
    expert_gate,
    expert_up,
    expert_down,
    projection,
    student_in,
    student_gain,
    student_gate,
    student_up,
    student_down,
):
    chips = lax.axis_size(CHIPS)
    projection_t = projection.T
    student_t = student_in.T

    arrived = exchange(dispatch(teacher_in, routes, student_t, student_gain[None, :]))
    expert_weights = (expert_gate[0], expert_up[0], expert_down[0])
    student_weights = (student_gate.T, student_up.T, student_down)
    here = student_t.shape[0]
    teacher_row = teacher_gain[None, :]
    routed = split(arrived, here, expert_weights + student_weights + (teacher_row,))
    routed_other = other_core(routed)
    first_pre, squares, cut = first_half(routed, teacher_row, *expert_weights[:2], projection_t)
    x_mine = split_student(arrived, here, routed_other, squares)
    x_other = other_core(x_mine)
    projection_other = other_core(cut)
    keep, send, token = experts(routed_other, first_pre, squares, teacher_row, *expert_weights)
    s_keep, s_send, act, pre, factor, x_all = forward(
        x_mine, x_other, routed, routed_other, *student_weights, token
    )
    outputs = merge(keep, other_core(send), projection_other)
    returned = exchange(outputs)
    joint = combine(returned, teacher_in, routes, gates, s_keep, other_core(s_send))
    near, far = targets(exchange(joint), projection_t, projection_other, student_t)
    d_mine = exchange(deltas(near, other_core(far), chips))
    d_other = other_core(d_mine)
    grad_gate, grad_up, grad_down, mse = backward(
        d_mine, d_other, x_all, student_down, act, pre, factor
    )
    return (grad_gate.T, grad_up.T, grad_down, mse.reshape(()))


def solution(mesh):
    everything = ("grp", "ep", "rep")
    placed = (
        P("ep", None),
        P(),
        P("ep", None),
        P("ep", None),
        P("ep", None, ("grp", "rep")),
        P("ep", None, ("grp", "rep")),
        P("ep", ("grp", "rep"), None),
        P(None, everything),
        P(None, everything),
        P(),
        P(None, everything),
        P(None, everything),
        P(everything, None),
    )
    return jax.shard_map(
        local,
        mesh=mesh,
        in_specs=placed,
        out_specs=(P(None, everything), P(None, everything), P(everything, None), P()),
        check_vma=False,
    )
```

```python
import math

import jax
import jax.numpy as jnp
from jax import lax
from jax.experimental import pallas as pl
from jax.experimental.pallas import tpu as pltpu
from jax.sharding import PartitionSpec as P

CHIPS = ("grp", "ep")
NN = (((1,), (0,)), ((), ()))
NT = (((1,), (1,)), ((), ()))
TN = (((0,), (0,)), ((), ()))
LANES = 128
PIECES = 4
SPARE = 16


def dot(a, b, dims=NN):
    return lax.dot_general(a, b, dims, preferred_element_type=jnp.float32)


def silu(v):
    return v / (1.0 + jnp.exp(-v))


def params(mebibytes):
    return pltpu.CompilerParams(vmem_limit_bytes=mebibytes * 1024 * 1024)


def cost(microseconds):
    flops = int(microseconds * 1e9)
    return pl.CostEstimate(flops=flops, bytes_accessed=0, transcendentals=0)


def vmem():
    return pl.BlockSpec(memory_space=pltpu.VMEM)


def anywhere():
    return pl.BlockSpec(memory_space=pl.ANY)


def in_hbm():
    return pl.BlockSpec(memory_space=pltpu.HBM)


def exchange(blocks):
    return lax.all_to_all(blocks, CHIPS, split_axis=0, concat_axis=0, tiled=True)


def other_core(values):
    return lax.ppermute(values, "rep", [(0, 1), (1, 0)])


def slot_weights(routes, gates, experts, copies):
    tokens, _ = routes.shape
    row = lax.broadcasted_iota(jnp.int32, (copies * experts * 2, routes.shape[1]), 0)
    expert, slot = (row // 2) % experts, (row % 2)[:, :1]
    earlier = jnp.zeros(slot.shape, jnp.float32)
    weights = []
    for t in range(tokens):
        hits = routes[t : t + 1, :] == expert
        taken = jnp.sum(jnp.where(hits, 1.0, 0.0), axis=1, keepdims=True)
        value = jnp.sum(jnp.where(hits, gates[t : t + 1, :], 0.0), axis=1, keepdims=True)
        weights.append(jnp.where(earlier == slot.astype(jnp.float32), value, 0.0))
        earlier += taken
    return weights


def padded_pieces(pieces):
    return -(-pieces // 8) * 8


def dispatch_kernel(
    tokens_hbm,
    routes_hbm,
    student_hbm,
    gain_hbm,
    out,
    rows,
    tokens,
    routes,
    student,
    gain,
    sems,
):
    chip = lax.axis_index("grp") * lax.axis_size("ep") + lax.axis_index("ep")
    mine = pl.ds(pl.multiple_of(chip * LANES, LANES), LANES)
    pairs = (
        (routes_hbm, routes),
        (tokens_hbm, tokens),
        (student_hbm, student),
        (gain_hbm.at[:, mine], gain),
    )
    copies_in = [pltpu.make_async_copy(a, b, sems.at[n]) for n, (a, b) in enumerate(pairs)]
    for copy in copies_in:
        copy.start()
    copies = lax.axis_size("grp")
    experts = lax.axis_size("ep")
    quarter = tokens.shape[1] // (copies * lax.axis_size("rep"))
    place = lax.axis_index("rep") * copies + lax.axis_index("grp")
    start = pl.multiple_of(place * quarter, quarter)
    pieces = quarter // LANES
    stride = padded_pieces(pieces)
    copies_in[2].wait()
    copies_in[3].wait()
    here = student.shape[0]
    values = student[...].astype(jnp.float32)
    squares = jnp.sum(values * values, axis=0, keepdims=True)
    high = squares.astype(jnp.bfloat16).astype(jnp.float32)
    for n, part in enumerate((high, squares - high)):
        rows[pl.ds(pieces + n, 2 * experts, stride=stride), :] = jnp.broadcast_to(
            part, (2 * experts, LANES)
        )
    columns = jnp.broadcast_to(gain[...], (LANES, LANES)).T
    columns = jnp.where(lax.axis_index("rep") == 0, columns[:here], columns[here:])
    block = (values * columns).astype(jnp.bfloat16)
    out[:, :here, :] = jnp.broadcast_to(block[None], (out.shape[0],) + block.shape)
    copies_in[0].wait()
    copies_in[1].wait()
    ids = routes[...]
    chosen = slot_weights(ids, jnp.ones(ids.shape, jnp.float32), experts, 1)
    for n in range(pieces):
        values = tokens[:, pl.ds(start + n * LANES, LANES)].astype(jnp.float32)
        picked = sum(c * values[t : t + 1, :] for t, c in enumerate(chosen))
        rows[pl.ds(n, 2 * experts, stride=stride), :] = picked
    whole = rows[: 2 * experts * stride, :]
    routed = whole.astype(jnp.bfloat16).reshape(experts, 2 * stride, LANES)
    for n in range(copies):
        out[n * experts : (n + 1) * experts, here:, :] = routed


def dispatch(tokens, routes, student, gain):
    copies, experts = lax.axis_size("grp"), lax.axis_size("ep")
    rows = 2 * padded_pieces(tokens.shape[1] // (copies * lax.axis_size("rep") * LANES))
    shape = (copies * experts, student.shape[0] + rows, LANES)
    return pl.pallas_call(
        dispatch_kernel,
        out_shape=jax.ShapeDtypeStruct(shape, jnp.bfloat16),
        in_specs=[in_hbm()] * 4,
        out_specs=vmem(),
        scratch_shapes=[
            pltpu.VMEM((experts * rows + SPARE, LANES), jnp.float32),
            pltpu.VMEM(tokens.shape, tokens.dtype),
            pltpu.VMEM(routes.shape, routes.dtype),
            pltpu.VMEM(student.shape, student.dtype),
            pltpu.VMEM((1, LANES), gain.dtype),
            pltpu.SemaphoreType.DMA((4,)),
        ],
        compiler_params=params(8),
        cost_estimate=cost(30),
        name="dispatch",
    )(
        *[
            pltpu.with_memory_space_constraint(a, pltpu.HBM)
            for a in (tokens, routes, student, gain)
        ]
    )


def scaled_tokens(source, gains, rows, scaled):
    routed = source.shape[0] * source.shape[1]
    groups = lax.axis_size("grp")
    slots, half = scaled.shape
    pieces = half // (groups * LANES)
    stride = padded_pieces(pieces)
    rows[:routed, :] = source.astype(jnp.float32).reshape(routed, LANES)
    squares = jnp.zeros((slots, LANES), jnp.float32)
    for g in range(groups):
        for m in range(pieces):
            column = (g * pieces + m) * LANES
            columns = slice(column, column + LANES)
            values = rows[pl.ds(g * slots * stride + m, slots, stride=stride), :]
            squares += values * values
            scaled[:, columns] = (values * gains[:, columns]).astype(jnp.bfloat16)
    return squares


def first_half_kernel(
    routed, gain, gate_w, up_w, projection, pre, squares, cut, rows, scaled, sem
):
    half = scaled.shape[1]
    core = lax.axis_index("rep")
    start = pl.multiple_of(core * half, half)
    cut_start = pl.multiple_of((1 - core) * half, half)
    copy = pltpu.make_async_copy(projection.at[:, pl.ds(cut_start, half)], cut, sem)
    copy.start()
    gains = gain[:, pl.ds(start, half)]
    squares[...] = scaled_tokens(routed[...], gains, rows, scaled)
    values = scaled[...]
    pre[0] = dot(values, gate_w[pl.ds(start, half), :])
    pre[1] = dot(values, up_w[pl.ds(start, half), :])
    copy.wait()


def first_half(routed, gain, gate, up, projection):
    slots = 2 * lax.axis_size("ep")
    half = gain.shape[1] // 2
    return pl.pallas_call(
        first_half_kernel,
        out_shape=(
            jax.ShapeDtypeStruct((2, slots, gate.shape[1]), jnp.float32),
            jax.ShapeDtypeStruct((slots, LANES), jnp.float32),
            jax.ShapeDtypeStruct((projection.shape[0], half), projection.dtype),
        ),
        in_specs=[vmem()] * 4 + [in_hbm()],
        out_specs=(vmem(),) * 3,
        scratch_shapes=[
            pltpu.VMEM((routed.shape[0] * routed.shape[1] + SPARE, LANES), jnp.float32),
            pltpu.VMEM((slots, half), jnp.bfloat16),
            pltpu.SemaphoreType.DMA,
        ],
        compiler_params=params(8),
        cost_estimate=cost(2),
        name="first_half",
    )(routed, gain, gate, up, pltpu.with_memory_space_constraint(projection, pltpu.HBM))


def expert_kernel(
    other, pre, squares, gain, gate_w, up_w, down_w, keep, send, token, rows, scaled, result
):
    slots, half = scaled.shape
    pieces = half // (lax.axis_size("grp") * LANES)
    stride = padded_pieces(pieces)
    core = lax.axis_index("rep")
    first = pl.multiple_of(core * half, half)
    second = pl.multiple_of((1 - core) * half, half)
    total = squares[...]
    total += scaled_tokens(other[...], gain[:, pl.ds(second, half)], rows, scaled)
    factor = lax.rsqrt(jnp.sum(total, axis=1, keepdims=True) / (2 * half) + 1e-05)
    token[...] = jnp.zeros(token.shape, token.dtype)
    values = scaled[...]
    gate_pre = (pre[0] + dot(values, gate_w[pl.ds(second, half), :])) * factor
    up_pre = (pre[1] + dot(values, up_w[pl.ds(second, half), :])) * factor
    hidden = (silu(gate_pre) * up_pre).astype(jnp.bfloat16)
    width = half // 2
    result[...] = jnp.zeros(result.shape, jnp.float32)
    for dst, start in ((send, second), (keep, first)):
        for n in range(2):
            columns = pl.ds(pl.multiple_of(start + n * width, width), width)
            out = dot(hidden, down_w[:, columns])
            for m in range(pieces):
                place = pl.ds(n * slots * stride + m, slots, stride=stride)
                result[place, :] = out[:, m * LANES : (m + 1) * LANES]
        dst[...] = result[: dst.shape[0], :].astype(dst.dtype)


def experts(other, pre, squares, gain, w_gate, w_up, w_down):
    groups, slots = lax.axis_size("grp"), squares.shape[0]
    half = gain.shape[1] // 2
    result = (groups * slots * padded_pieces(half // (groups * LANES)), LANES)
    return pl.pallas_call(
        expert_kernel,
        out_shape=(
            jax.ShapeDtypeStruct(result, jnp.float32),
            jax.ShapeDtypeStruct(result, jnp.bfloat16),
            jax.ShapeDtypeStruct((8, LANES), jnp.float32),
        ),
        in_specs=[vmem()] * 7,
        out_specs=(vmem(),) * 3,
        scratch_shapes=[
            pltpu.VMEM((result[0] + SPARE, LANES), jnp.float32),
            pltpu.VMEM((slots, half), jnp.bfloat16),
            pltpu.VMEM((result[0] + SPARE, LANES), jnp.float32),
        ],
        compiler_params=params(8),
        cost_estimate=cost(3),
        name="experts",
    )(other, pre, squares, gain, w_gate, w_up, w_down)


def combine_kernel(returned, tokens, routes, gates, keep, received, out, rows, own):
    copies = lax.axis_size("grp")
    experts = lax.axis_size("ep")
    slots = 2 * copies * experts
    stride = returned.shape[0] // slots
    quarter = tokens.shape[1] // (copies * lax.axis_size("rep"))
    pieces = quarter // LANES
    place = lax.axis_index("rep") * copies + lax.axis_index("grp")
    start = pl.multiple_of(place * quarter, quarter)
    count = tokens.shape[0]
    weights = slot_weights(routes[...], gates[...], experts, copies)
    weights = [jnp.broadcast_to(w, (slots, LANES)) for w in weights]
    rows[: returned.shape[0], :] = returned[...].astype(jnp.float32)
    for m in range(pieces):
        values = rows[pl.ds(m, slots, stride=stride), :]
        before = tokens[:, pl.ds(start + m * LANES, LANES)].astype(jnp.float32)
        for t in range(count):
            moe = jnp.sum(values * weights[t], axis=0, keepdims=True)
            own[t * pieces + m : t * pieces + m + 1, :] = before[t : t + 1, :] + moe
    here = keep.shape[1]
    block = own[...].astype(jnp.bfloat16)
    out[:, :here, :] = (keep[...] + received[...].astype(jnp.float32)).astype(jnp.bfloat16)
    out[:, here:, :] = jnp.broadcast_to(block[None], (out.shape[0],) + block.shape)


def combine(returned, tokens, routes, gates, keep, received):
    chips, rows, _ = keep.shape
    own = tokens.size // (lax.axis_size("grp") * lax.axis_size("rep") * LANES)
    return pl.pallas_call(
        combine_kernel,
        out_shape=jax.ShapeDtypeStruct((chips, rows + own, LANES), jnp.bfloat16),
        in_specs=[vmem()] * 6,
        out_specs=vmem(),
        scratch_shapes=[
            pltpu.VMEM((returned.shape[0] + SPARE, LANES), jnp.float32),
            pltpu.VMEM((own, LANES), jnp.float32),
        ],
        compiler_params=params(16),
        cost_estimate=cost(4),
        name="combine",
    )(returned, tokens, routes, gates, keep, received)


def split_kernel(arrived, *refs):
    routed = refs[-1]
    routed[...] = arrived[:, arrived.shape[1] - routed.shape[1] :, :]


def split(arrived, rows, weights):
    chips, total, lanes = arrived.shape
    return pl.pallas_call(
        split_kernel,
        out_shape=jax.ShapeDtypeStruct((chips, total - rows, lanes), arrived.dtype),
        in_specs=[vmem()] * (1 + len(weights)),
        out_specs=vmem(),
        compiler_params=params(4),
        cost_estimate=cost(1),
        name="split",
    )(arrived, *weights)


def split_student_kernel(arrived, other, squares, student):
    del other, squares
    student[...] = arrived[:, : student.shape[1], :]


def split_student(arrived, rows, *after):
    chips, _, lanes = arrived.shape
    return pl.pallas_call(
        split_student_kernel,
        out_shape=jax.ShapeDtypeStruct((chips, rows, lanes), arrived.dtype),
        in_specs=[vmem()] + [anywhere()] * 2,
        out_specs=vmem(),
        compiler_params=params(4),
        cost_estimate=cost(1),
        name="split_student",
    )(arrived, *after)


def merge_kernel(keep, received, after, out):
    out[...] = (keep[...] + received[...].astype(jnp.float32)).astype(out.dtype)


def merge(keep, received, after):
    return pl.pallas_call(
        merge_kernel,
        out_shape=jax.ShapeDtypeStruct(received.shape, received.dtype),
        in_specs=[vmem()] * 2 + [anywhere()],
        out_specs=vmem(),
        compiler_params=params(6),
        cost_estimate=cost(1),
        name="merge",
    )(keep, received, after)


def start_interleaved(mine, other, dst, sems):
    core = lax.axis_index("rep")
    size = dst.shape[0] // PIECES
    copies = []
    for n in range(PIECES):
        here = pl.ds(n * size, size)
        for m, (src, to) in enumerate(((mine, core), (other, 1 - core))):
            copies.append(pltpu.make_async_copy(src.at[here], dst.at[here, to], sems.at[m, n]))
    for copy in copies:
        copy.start()
    return copies


def forward_kernel(mine, other, routed, routed_other, gate, up, down, after, keep, *refs):
    send, act_ref, pre_ref, factor_ref, x, sems = refs
    core = lax.axis_index("rep")
    chips, cores, rows, tokens = x.shape
    features = chips * cores * rows
    hidden = down.shape[0]
    copies = start_interleaved(mine, other, x, sems)
    stride = routed.shape[1] // 2
    sums = jnp.zeros((1, tokens), jnp.float32)
    for part in (routed, routed_other):
        rows_of = part[:, stride - 2 : stride, :].astype(jnp.float32)
        sums += jnp.sum(jnp.sum(rows_of, axis=0), axis=0, keepdims=True)
    factor = lax.rsqrt(sums / features + 1e-05)
    factor_ref[...] = factor
    for copy in copies:
        copy.wait()
    values = x[...].reshape(features, tokens)
    pre_ref[:hidden, :] = dot(gate[...], values) * factor
    pre_ref[hidden:, :] = dot(up[...], values) * factor
    pre = pre_ref[...]
    act = (silu(pre[:hidden]) * pre[hidden:]).astype(jnp.bfloat16)
    act_ref[...] = act
    step = 8
    width = step * 2 * rows
    for n in range(chips // step):
        part = dot(down[:, n * width : (n + 1) * width], act, TN).reshape(step, 2, rows, tokens)
        here = slice(n * step, (n + 1) * step)
        low, high = part[:, 0], part[:, 1]
        keep[here] = jnp.where(core == 0, low, high)
        send[here] = jnp.where(core == 0, high, low).astype(jnp.bfloat16)


def forward(mine, other, routed, routed_other, gate, up, down, after):
    chips, _, tokens = mine.shape
    hidden, features = down.shape
    rows = features // (2 * chips)
    whole = (chips, 2, rows, tokens)
    return pl.pallas_call(
        forward_kernel,
        out_shape=(
            jax.ShapeDtypeStruct((chips, rows, tokens), jnp.float32),
            jax.ShapeDtypeStruct((chips, rows, tokens), jnp.bfloat16),
            jax.ShapeDtypeStruct((hidden, tokens), jnp.bfloat16),
            jax.ShapeDtypeStruct((2 * hidden, tokens), jnp.float32),
            jax.ShapeDtypeStruct((1, tokens), jnp.float32),
            jax.ShapeDtypeStruct(whole, jnp.bfloat16),
        ),
        in_specs=[anywhere()] * 2 + [vmem()] * 5 + [anywhere()],
        out_specs=(vmem(),) * 6,
        scratch_shapes=[pltpu.SemaphoreType.DMA((2, PIECES))],
        compiler_params=params(20),
        cost_estimate=cost(8),
        name="forward",
    )(mine, other, routed, routed_other, gate, up, down, after)


def target_kernel(arrived, projection, projection_other, student_in, near, far, rows, tokens):
    here = student_in.shape[0]
    chips, total, lanes = arrived.shape
    count, half = tokens.shape
    groups = lax.axis_size("grp")
    pieces = half // (groups * lanes)
    start = pl.multiple_of(lax.axis_index("rep") * half, half)
    whole = chips * (total - here)
    rows[:whole, :] = arrived[:, here:, :].astype(jnp.float32).reshape(whole, lanes)
    for g in range(groups):
        for m in range(pieces):
            place = pl.ds(g * count * pieces + m, count, stride=pieces)
            columns = slice((g * pieces + m) * lanes, (g * pieces + m + 1) * lanes)
            tokens[:, columns] = rows[place, :].astype(jnp.bfloat16)
    values = tokens[...]
    far[...] = dot(projection_other[...], values, NT)
    branch = jnp.sum(arrived[:, :here, :].astype(jnp.float32), axis=0)
    target = dot(projection[:, pl.ds(start, half)], values, NT)
    near[...] = student_in[...].astype(jnp.float32) + branch - target


def targets(arrived, projection, projection_other, student_in):
    here, count = student_in.shape
    chips, total, lanes = arrived.shape
    half = projection_other.shape[1]
    part = jax.ShapeDtypeStruct((here, count), jnp.float32)
    return pl.pallas_call(
        target_kernel,
        out_shape=(part, part),
        in_specs=[vmem()] * 4,
        out_specs=(vmem(),) * 2,
        scratch_shapes=[
            pltpu.VMEM((chips * (total - here) + SPARE, lanes), jnp.float32),
            pltpu.VMEM((count, half), jnp.bfloat16),
        ],
        compiler_params=params(16),
        cost_estimate=cost(4),
        name="targets",
    )(arrived, projection, projection_other, student_in)


def delta_kernel(near, far, delta):
    tokens = near.shape[1]
    scaled = ((near[...] - far[...]) / math.sqrt(tokens)).astype(jnp.bfloat16)
    delta[...] = jnp.broadcast_to(scaled[None], delta.shape)


def deltas(near, far, chips):
    return pl.pallas_call(
        delta_kernel,
        out_shape=jax.ShapeDtypeStruct((chips,) + near.shape, jnp.bfloat16),
        in_specs=[vmem()] * 2,
        out_specs=vmem(),
        compiler_params=params(4),
        cost_estimate=cost(1),
        name="deltas",
    )(near, far)


def backward_kernel(
    d_mine,
    d_other,
    x,
    down,
    act,
    pre,
    factor,
    grad_gate_hbm,
    grad_up_hbm,
    grad_down_hbm,
    mse,
    d,
    grad_gate,
    grad_up,
    grad_down,
    sems_d,
    sems_out,
):
    chips, _, rows, tokens = d.shape
    features = chips * 2 * rows
    copies_d = start_interleaved(d_mine, d_other, d, sems_d)
    for copy in copies_d:
        copy.wait()
    hidden = act.shape[0]
    delta = d[...].reshape(features, tokens)
    back = dot(down[...], delta)
    gate_pre, up_pre = pre[:hidden], pre[hidden:]
    sigmoid = 1.0 / (1.0 + jnp.exp(-gate_pre))
    d_gate = back * up_pre * sigmoid * (1.0 + gate_pre * (1.0 - sigmoid))
    d_up = back * gate_pre * sigmoid
    scale = factor[...]
    d_both = jnp.concatenate([d_gate * scale, d_up * scale], axis=0).astype(jnp.bfloat16)
    step = 8
    width = step * 2 * rows
    acts = act[...]
    copies = []

    def send_out(kind, n, src, dst):
        here = slice(n * width, (n + 1) * width)
        copy = pltpu.make_async_copy(src.at[:, here], dst.at[:, here], sems_out.at[kind, n])
        copy.start()
        copies.append(copy)

    total = jnp.zeros((1, tokens), jnp.float32)
    for n in range(chips // step):
        here = slice(n * width, (n + 1) * width)
        part = d[n * step : (n + 1) * step].reshape(width, tokens)
        grad_down[:, here] = dot(acts, part, NT).astype(jnp.bfloat16)
        send_out(0, n, grad_down, grad_down_hbm)
        floats = part.astype(jnp.float32)
        total += jnp.sum(floats * floats, axis=0, keepdims=True)
    mse[...] = jnp.sum(total, axis=1, keepdims=True) / features
    for n in range(chips // step):
        here = slice(n * width, (n + 1) * width)
        part = x[n * step : (n + 1) * step].reshape(width, tokens)
        grads = dot(d_both, part, NT)
        grad_gate[:, here] = grads[:hidden].astype(jnp.bfloat16)
        grad_up[:, here] = grads[hidden:].astype(jnp.bfloat16)
        send_out(1, n, grad_gate, grad_gate_hbm)
        send_out(2, n, grad_up, grad_up_hbm)
    for copy in copies:
        copy.wait()


def backward(d_mine, d_other, x, down, act, pre, factor):
    chips, rows, tokens = d_mine.shape
    hidden, features = down.shape
    grad = jax.ShapeDtypeStruct((hidden, features), jnp.bfloat16)
    whole = pltpu.VMEM((chips, 2, rows, tokens), jnp.bfloat16)
    return pl.pallas_call(
        backward_kernel,
        out_shape=(grad, grad, grad, jax.ShapeDtypeStruct((1, 1), jnp.float32)),
        in_specs=[anywhere()] * 2 + [vmem()] * 5,
        out_specs=(anywhere(),) * 3 + (vmem(),),
        scratch_shapes=[
            whole,
            *[pltpu.VMEM((hidden, features), jnp.bfloat16)] * 3,
            pltpu.SemaphoreType.DMA((2, PIECES)),
            pltpu.SemaphoreType.DMA((3, 8)),
        ],
        compiler_params=params(24),
        cost_estimate=cost(8),
        name="backward",
    )(d_mine, d_other, x, down, act, pre, factor)


def local(
    teacher_in,
    teacher_gain,
    routes,
    gates,
    expert_gate,
    expert_up,
    expert_down,
    projection,
    student_in,
    student_gain,
    student_gate,
    student_up,
    student_down,
):
    chips = lax.axis_size(CHIPS)
    projection_t = projection.T
    student_t = student_in.T

    arrived = exchange(dispatch(teacher_in, routes, student_t, student_gain[None, :]))
    expert_weights = (expert_gate[0], expert_up[0], expert_down[0])
    student_weights = (student_gate.T, student_up.T, student_down)
    here = student_t.shape[0]
    teacher_row = teacher_gain[None, :]
    routed = split(arrived, here, expert_weights + student_weights + (teacher_row,))
    routed_other = other_core(routed)
    first_pre, squares, cut = first_half(routed, teacher_row, *expert_weights[:2], projection_t)
    x_mine = split_student(arrived, here, routed_other, squares)
    x_other = other_core(x_mine)
    projection_other = other_core(cut)
    keep, send, token = experts(routed_other, first_pre, squares, teacher_row, *expert_weights)
    s_keep, s_send, act, pre, factor, x_all = forward(
        x_mine, x_other, routed, routed_other, *student_weights, token
    )
    outputs = merge(keep, other_core(send), projection_other)
    returned = exchange(outputs)
    joint = combine(returned, teacher_in, routes, gates, s_keep, other_core(s_send))
    near, far = targets(exchange(joint), projection_t, projection_other, student_t)
    d_mine = exchange(deltas(near, other_core(far), chips))
    d_other = other_core(d_mine)
    grad_gate, grad_up, grad_down, mse = backward(
        d_mine, d_other, x_all, student_down, act, pre, factor
    )
    return (grad_gate.T, grad_up.T, grad_down, mse.reshape(()))


def solution(mesh):
    everything = ("grp", "ep", "rep")
    placed = (
        P("ep", None),
        P(),
        P("ep", None),
        P("ep", None),
        P("ep", None, ("grp", "rep")),
        P("ep", None, ("grp", "rep")),
        P("ep", ("grp", "rep"), None),
        P(None, everything),
        P(None, everything),
        P(),
        P(None, everything),
        P(None, everything),
        P(everything, None),
    )
    return jax.shard_map(
        local,
        mesh=mesh,
        in_specs=placed,
        out_specs=(P(None, everything), P(None, everything), P(everything, None), P()),
        check_vma=False,
    )
```

```python
import math

import jax
import jax.numpy as jnp
from jax import lax
from jax.experimental import pallas as pl
from jax.experimental.pallas import tpu as pltpu
from jax.sharding import PartitionSpec as P

CHIPS = ("grp", "ep")
NN = (((1,), (0,)), ((), ()))
NT = (((1,), (1,)), ((), ()))
TN = (((0,), (0,)), ((), ()))
LANES = 128
PIECES = 8
SPARE = 16


def dot(a, b, dims=NN):
    return lax.dot_general(a, b, dims, preferred_element_type=jnp.float32)


def silu(v):
    return v / (1.0 + jnp.exp(-v))


def params(mebibytes):
    return pltpu.CompilerParams(vmem_limit_bytes=mebibytes * 1024 * 1024)


def cost(microseconds):
    flops = int(microseconds * 1e9)
    return pl.CostEstimate(flops=flops, bytes_accessed=0, transcendentals=0)


def vmem():
    return pl.BlockSpec(memory_space=pltpu.VMEM)


def anywhere():
    return pl.BlockSpec(memory_space=pl.ANY)


def in_hbm():
    return pl.BlockSpec(memory_space=pltpu.HBM)


def exchange(blocks):
    return lax.all_to_all(blocks, CHIPS, split_axis=0, concat_axis=0, tiled=True)


def other_core(values):
    return lax.ppermute(values, "rep", [(0, 1), (1, 0)])


def slot_weights(routes, gates, experts, copies):
    tokens, _ = routes.shape
    row = lax.broadcasted_iota(jnp.int32, (copies * experts * 2, routes.shape[1]), 0)
    expert, slot = (row // 2) % experts, (row % 2)[:, :1]
    earlier = jnp.zeros(slot.shape, jnp.float32)
    weights = []
    for t in range(tokens):
        hits = routes[t : t + 1, :] == expert
        taken = jnp.sum(jnp.where(hits, 1.0, 0.0), axis=1, keepdims=True)
        value = jnp.sum(jnp.where(hits, gates[t : t + 1, :], 0.0), axis=1, keepdims=True)
        weights.append(jnp.where(earlier == slot.astype(jnp.float32), value, 0.0))
        earlier += taken
    return weights


def padded_pieces(pieces):
    return -(-pieces // 8) * 8


def dispatch_kernel(
    tokens_hbm,
    routes_hbm,
    student_hbm,
    gain_hbm,
    out,
    rows,
    tokens,
    routes,
    student,
    gain,
    sems,
):
    chip = lax.axis_index("grp") * lax.axis_size("ep") + lax.axis_index("ep")
    mine = pl.ds(pl.multiple_of(chip * LANES, LANES), LANES)
    pairs = (
        (routes_hbm, routes),
        (tokens_hbm, tokens),
        (student_hbm, student),
        (gain_hbm.at[:, mine], gain),
    )
    copies_in = [pltpu.make_async_copy(a, b, sems.at[n]) for n, (a, b) in enumerate(pairs)]
    for copy in copies_in:
        copy.start()
    copies = lax.axis_size("grp")
    experts = lax.axis_size("ep")
    quarter = tokens.shape[1] // (copies * lax.axis_size("rep"))
    place = lax.axis_index("rep") * copies + lax.axis_index("grp")
    start = pl.multiple_of(place * quarter, quarter)
    pieces = quarter // LANES
    stride = padded_pieces(pieces)
    copies_in[2].wait()
    copies_in[3].wait()
    here = student.shape[0]
    values = student[...].astype(jnp.float32)
    squares = jnp.sum(values * values, axis=0, keepdims=True)
    high = squares.astype(jnp.bfloat16).astype(jnp.float32)
    for n, part in enumerate((high, squares - high)):
        rows[pl.ds(pieces + n, 2 * experts, stride=stride), :] = jnp.broadcast_to(
            part, (2 * experts, LANES)
        )
    columns = jnp.broadcast_to(gain[...], (LANES, LANES)).T
    columns = jnp.where(lax.axis_index("rep") == 0, columns[:here], columns[here:])
    block = (values * columns).astype(jnp.bfloat16)
    out[:, :here, :] = jnp.broadcast_to(block[None], (out.shape[0],) + block.shape)
    copies_in[0].wait()
    copies_in[1].wait()
    ids = routes[...]
    chosen = slot_weights(ids, jnp.ones(ids.shape, jnp.float32), experts, 1)
    for n in range(pieces):
        values = tokens[:, pl.ds(start + n * LANES, LANES)].astype(jnp.float32)
        picked = sum(c * values[t : t + 1, :] for t, c in enumerate(chosen))
        rows[pl.ds(n, 2 * experts, stride=stride), :] = picked
    whole = rows[: 2 * experts * stride, :]
    routed = whole.astype(jnp.bfloat16).reshape(experts, 2 * stride, LANES)
    for n in range(copies):
        out[n * experts : (n + 1) * experts, here:, :] = routed


def dispatch(tokens, routes, student, gain):
    copies, experts = lax.axis_size("grp"), lax.axis_size("ep")
    rows = 2 * padded_pieces(tokens.shape[1] // (copies * lax.axis_size("rep") * LANES))
    shape = (copies * experts, student.shape[0] + rows, LANES)
    return pl.pallas_call(
        dispatch_kernel,
        out_shape=jax.ShapeDtypeStruct(shape, jnp.bfloat16),
        in_specs=[in_hbm()] * 4,
        out_specs=vmem(),
        scratch_shapes=[
            pltpu.VMEM((experts * rows + SPARE, LANES), jnp.float32),
            pltpu.VMEM(tokens.shape, tokens.dtype),
            pltpu.VMEM(routes.shape, routes.dtype),
            pltpu.VMEM(student.shape, student.dtype),
            pltpu.VMEM((1, LANES), gain.dtype),
            pltpu.SemaphoreType.DMA((4,)),
        ],
        compiler_params=params(8),
        cost_estimate=cost(30),
        name="dispatch",
    )(
        *[
            pltpu.with_memory_space_constraint(a, pltpu.HBM)
            for a in (tokens, routes, student, gain)
        ]
    )


def scaled_tokens(source, gains, rows, scaled):
    routed = source.shape[0] * source.shape[1]
    groups = lax.axis_size("grp")
    slots, half = scaled.shape
    pieces = half // (groups * LANES)
    stride = padded_pieces(pieces)
    rows[:routed, :] = source.astype(jnp.float32).reshape(routed, LANES)
    squares = jnp.zeros((slots, LANES), jnp.float32)
    for g in range(groups):
        for m in range(pieces):
            column = (g * pieces + m) * LANES
            columns = slice(column, column + LANES)
            values = rows[pl.ds(g * slots * stride + m, slots, stride=stride), :]
            squares += values * values
            scaled[:, columns] = (values * gains[:, columns]).astype(jnp.bfloat16)
    return squares


def first_half_kernel(
    routed, gain, gate_w, up_w, projection, pre, squares, cut, rows, scaled, sem
):
    half = scaled.shape[1]
    core = lax.axis_index("rep")
    start = pl.multiple_of(core * half, half)
    cut_start = pl.multiple_of((1 - core) * half, half)
    copy = pltpu.make_async_copy(projection.at[:, pl.ds(cut_start, half)], cut, sem)
    copy.start()
    gains = gain[:, pl.ds(start, half)]
    squares[...] = scaled_tokens(routed[...], gains, rows, scaled)
    values = scaled[...]
    pre[0] = dot(values, gate_w[pl.ds(start, half), :])
    pre[1] = dot(values, up_w[pl.ds(start, half), :])
    copy.wait()


def first_half(routed, gain, gate, up, projection):
    slots = 2 * lax.axis_size("ep")
    half = gain.shape[1] // 2
    return pl.pallas_call(
        first_half_kernel,
        out_shape=(
            jax.ShapeDtypeStruct((2, slots, gate.shape[1]), jnp.float32),
            jax.ShapeDtypeStruct((slots, LANES), jnp.float32),
            jax.ShapeDtypeStruct((projection.shape[0], half), projection.dtype),
        ),
        in_specs=[vmem()] * 4 + [in_hbm()],
        out_specs=(vmem(),) * 3,
        scratch_shapes=[
            pltpu.VMEM((routed.shape[0] * routed.shape[1] + SPARE, LANES), jnp.float32),
            pltpu.VMEM((slots, half), jnp.bfloat16),
            pltpu.SemaphoreType.DMA,
        ],
        compiler_params=params(8),
        cost_estimate=cost(2),
        name="first_half",
    )(routed, gain, gate, up, pltpu.with_memory_space_constraint(projection, pltpu.HBM))


def expert_kernel(
    other, pre, squares, gain, gate_w, up_w, down_w, keep, send, token, rows, scaled, result
):
    slots, half = scaled.shape
    pieces = half // (lax.axis_size("grp") * LANES)
    stride = padded_pieces(pieces)
    core = lax.axis_index("rep")
    first = pl.multiple_of(core * half, half)
    second = pl.multiple_of((1 - core) * half, half)
    total = squares[...]
    total += scaled_tokens(other[...], gain[:, pl.ds(second, half)], rows, scaled)
    factor = lax.rsqrt(jnp.sum(total, axis=1, keepdims=True) / (2 * half) + 1e-05)
    token[...] = jnp.zeros(token.shape, token.dtype)
    values = scaled[...]
    gate_pre = (pre[0] + dot(values, gate_w[pl.ds(second, half), :])) * factor
    up_pre = (pre[1] + dot(values, up_w[pl.ds(second, half), :])) * factor
    hidden = (silu(gate_pre) * up_pre).astype(jnp.bfloat16)
    width = half // 2
    result[...] = jnp.zeros(result.shape, jnp.float32)
    for dst, start in ((send, second), (keep, first)):
        for n in range(2):
            columns = pl.ds(pl.multiple_of(start + n * width, width), width)
            out = dot(hidden, down_w[:, columns])
            for m in range(pieces):
                place = pl.ds(n * slots * stride + m, slots, stride=stride)
                result[place, :] = out[:, m * LANES : (m + 1) * LANES]
        dst[...] = result[: dst.shape[0], :].astype(dst.dtype)


def experts(other, pre, squares, gain, w_gate, w_up, w_down):
    groups, slots = lax.axis_size("grp"), squares.shape[0]
    half = gain.shape[1] // 2
    result = (groups * slots * padded_pieces(half // (groups * LANES)), LANES)
    return pl.pallas_call(
        expert_kernel,
        out_shape=(
            jax.ShapeDtypeStruct(result, jnp.float32),
            jax.ShapeDtypeStruct(result, jnp.bfloat16),
            jax.ShapeDtypeStruct((8, LANES), jnp.float32),
        ),
        in_specs=[vmem()] * 7,
        out_specs=(vmem(),) * 3,
        scratch_shapes=[
            pltpu.VMEM((result[0] + SPARE, LANES), jnp.float32),
            pltpu.VMEM((slots, half), jnp.bfloat16),
            pltpu.VMEM((result[0] + SPARE, LANES), jnp.float32),
        ],
        compiler_params=params(8),
        cost_estimate=cost(3),
        name="experts",
    )(other, pre, squares, gain, w_gate, w_up, w_down)


def combine_kernel(returned, tokens, routes, gates, keep, received, out, rows, own):
    copies = lax.axis_size("grp")
    experts = lax.axis_size("ep")
    slots = 2 * copies * experts
    stride = returned.shape[0] // slots
    quarter = tokens.shape[1] // (copies * lax.axis_size("rep"))
    pieces = quarter // LANES
    place = lax.axis_index("rep") * copies + lax.axis_index("grp")
    start = pl.multiple_of(place * quarter, quarter)
    count = tokens.shape[0]
    weights = slot_weights(routes[...], gates[...], experts, copies)
    weights = [jnp.broadcast_to(w, (slots, LANES)) for w in weights]
    rows[: returned.shape[0], :] = returned[...].astype(jnp.float32)
    for m in range(pieces):
        values = rows[pl.ds(m, slots, stride=stride), :]
        before = tokens[:, pl.ds(start + m * LANES, LANES)].astype(jnp.float32)
        for t in range(count):
            moe = jnp.sum(values * weights[t], axis=0, keepdims=True)
            own[t * pieces + m : t * pieces + m + 1, :] = before[t : t + 1, :] + moe
    here = keep.shape[1]
    block = own[...].astype(jnp.bfloat16)
    out[:, :here, :] = (keep[...] + received[...].astype(jnp.float32)).astype(jnp.bfloat16)
    out[:, here:, :] = jnp.broadcast_to(block[None], (out.shape[0],) + block.shape)


def combine(returned, tokens, routes, gates, keep, received):
    chips, rows, _ = keep.shape
    own = tokens.size // (lax.axis_size("grp") * lax.axis_size("rep") * LANES)
    return pl.pallas_call(
        combine_kernel,
        out_shape=jax.ShapeDtypeStruct((chips, rows + own, LANES), jnp.bfloat16),
        in_specs=[vmem()] * 6,
        out_specs=vmem(),
        scratch_shapes=[
            pltpu.VMEM((returned.shape[0] + SPARE, LANES), jnp.float32),
            pltpu.VMEM((own, LANES), jnp.float32),
        ],
        compiler_params=params(16),
        cost_estimate=cost(4),
        name="combine",
    )(returned, tokens, routes, gates, keep, received)


def split_kernel(arrived, *refs):
    routed = refs[-1]
    routed[...] = arrived[:, arrived.shape[1] - routed.shape[1] :, :]


def split(arrived, rows, weights):
    chips, total, lanes = arrived.shape
    return pl.pallas_call(
        split_kernel,
        out_shape=jax.ShapeDtypeStruct((chips, total - rows, lanes), arrived.dtype),
        in_specs=[vmem()] * (1 + len(weights)),
        out_specs=vmem(),
        compiler_params=params(4),
        cost_estimate=cost(1),
        name="split",
    )(arrived, *weights)


def split_student_kernel(arrived, other, squares, student):
    del other, squares
    student[...] = arrived[:, : student.shape[1], :]


def split_student(arrived, rows, *after):
    chips, _, lanes = arrived.shape
    return pl.pallas_call(
        split_student_kernel,
        out_shape=jax.ShapeDtypeStruct((chips, rows, lanes), arrived.dtype),
        in_specs=[vmem()] + [anywhere()] * 2,
        out_specs=vmem(),
        compiler_params=params(4),
        cost_estimate=cost(1),
        name="split_student",
    )(arrived, *after)


def merge_kernel(keep, received, after, out):
    out[...] = (keep[...] + received[...].astype(jnp.float32)).astype(out.dtype)


def merge(keep, received, after):
    return pl.pallas_call(
        merge_kernel,
        out_shape=jax.ShapeDtypeStruct(received.shape, received.dtype),
        in_specs=[vmem()] * 2 + [anywhere()],
        out_specs=vmem(),
        compiler_params=params(6),
        cost_estimate=cost(1),
        name="merge",
    )(keep, received, after)


def start_interleaved(mine, other, dst, sems):
    core = lax.axis_index("rep")
    size = dst.shape[0] // PIECES
    copies = []
    for n in range(PIECES):
        here = pl.ds(n * size, size)
        for m, (src, to) in enumerate(((mine, core), (other, 1 - core))):
            copies.append(pltpu.make_async_copy(src.at[here], dst.at[here, to], sems.at[m, n]))
    for copy in copies:
        copy.start()
    return copies


def forward_kernel(mine, other, routed, routed_other, gate, up, down, after, keep, *refs):
    send, act_ref, pre_ref, factor_ref, x, sems = refs
    core = lax.axis_index("rep")
    chips, cores, rows, tokens = x.shape
    features = chips * cores * rows
    hidden = down.shape[0]
    copies = start_interleaved(mine, other, x, sems)
    stride = routed.shape[1] // 2
    sums = jnp.zeros((1, tokens), jnp.float32)
    for part in (routed, routed_other):
        rows_of = part[:, stride - 2 : stride, :].astype(jnp.float32)
        sums += jnp.sum(jnp.sum(rows_of, axis=0), axis=0, keepdims=True)
    factor = lax.rsqrt(sums / features + 1e-05)
    factor_ref[...] = factor
    for copy in copies:
        copy.wait()
    values = x[...].reshape(features, tokens)
    pre_ref[:hidden, :] = dot(gate[...], values) * factor
    pre_ref[hidden:, :] = dot(up[...], values) * factor
    pre = pre_ref[...]
    act = (silu(pre[:hidden]) * pre[hidden:]).astype(jnp.bfloat16)
    act_ref[...] = act
    step = 8
    width = step * 2 * rows
    for n in range(chips // step):
        part = dot(down[:, n * width : (n + 1) * width], act, TN).reshape(step, 2, rows, tokens)
        here = slice(n * step, (n + 1) * step)
        low, high = part[:, 0], part[:, 1]
        keep[here] = jnp.where(core == 0, low, high)
        send[here] = jnp.where(core == 0, high, low).astype(jnp.bfloat16)


def forward(mine, other, routed, routed_other, gate, up, down, after):
    chips, _, tokens = mine.shape
    hidden, features = down.shape
    rows = features // (2 * chips)
    whole = (chips, 2, rows, tokens)
    return pl.pallas_call(
        forward_kernel,
        out_shape=(
            jax.ShapeDtypeStruct((chips, rows, tokens), jnp.float32),
            jax.ShapeDtypeStruct((chips, rows, tokens), jnp.bfloat16),
            jax.ShapeDtypeStruct((hidden, tokens), jnp.bfloat16),
            jax.ShapeDtypeStruct((2 * hidden, tokens), jnp.float32),
            jax.ShapeDtypeStruct((1, tokens), jnp.float32),
            jax.ShapeDtypeStruct(whole, jnp.bfloat16),
        ),
        in_specs=[anywhere()] * 2 + [vmem()] * 5 + [anywhere()],
        out_specs=(vmem(),) * 6,
        scratch_shapes=[pltpu.SemaphoreType.DMA((2, PIECES))],
        compiler_params=params(20),
        cost_estimate=cost(8),
        name="forward",
    )(mine, other, routed, routed_other, gate, up, down, after)


def target_kernel(arrived, projection, projection_other, student_in, near, far, rows, tokens):
    here = student_in.shape[0]
    chips, total, lanes = arrived.shape
    count, half = tokens.shape
    groups = lax.axis_size("grp")
    pieces = half // (groups * lanes)
    start = pl.multiple_of(lax.axis_index("rep") * half, half)
    whole = chips * (total - here)
    rows[:whole, :] = arrived[:, here:, :].astype(jnp.float32).reshape(whole, lanes)
    for g in range(groups):
        for m in range(pieces):
            place = pl.ds(g * count * pieces + m, count, stride=pieces)
            columns = slice((g * pieces + m) * lanes, (g * pieces + m + 1) * lanes)
            tokens[:, columns] = rows[place, :].astype(jnp.bfloat16)
    values = tokens[...]
    far[...] = dot(projection_other[...], values, NT)
    branch = jnp.sum(arrived[:, :here, :].astype(jnp.float32), axis=0)
    target = dot(projection[:, pl.ds(start, half)], values, NT)
    near[...] = student_in[...].astype(jnp.float32) + branch - target


def targets(arrived, projection, projection_other, student_in):
    here, count = student_in.shape
    chips, total, lanes = arrived.shape
    half = projection_other.shape[1]
    part = jax.ShapeDtypeStruct((here, count), jnp.float32)
    return pl.pallas_call(
        target_kernel,
        out_shape=(part, part),
        in_specs=[vmem()] * 4,
        out_specs=(vmem(),) * 2,
        scratch_shapes=[
            pltpu.VMEM((chips * (total - here) + SPARE, lanes), jnp.float32),
            pltpu.VMEM((count, half), jnp.bfloat16),
        ],
        compiler_params=params(16),
        cost_estimate=cost(4),
        name="targets",
    )(arrived, projection, projection_other, student_in)


def delta_kernel(near, far, delta):
    tokens = near.shape[1]
    scaled = ((near[...] - far[...]) / math.sqrt(tokens)).astype(jnp.bfloat16)
    delta[...] = jnp.broadcast_to(scaled[None], delta.shape)


def deltas(near, far, chips):
    return pl.pallas_call(
        delta_kernel,
        out_shape=jax.ShapeDtypeStruct((chips,) + near.shape, jnp.bfloat16),
        in_specs=[vmem()] * 2,
        out_specs=vmem(),
        compiler_params=params(4),
        cost_estimate=cost(1),
        name="deltas",
    )(near, far)


def backward_kernel(
    d_mine,
    d_other,
    x,
    down,
    act,
    pre,
    factor,
    grad_gate_hbm,
    grad_up_hbm,
    grad_down_hbm,
    mse,
    d,
    grad_gate,
    grad_up,
    grad_down,
    sems_d,
    sems_out,
):
    chips, _, rows, tokens = d.shape
    features = chips * 2 * rows
    copies_d = start_interleaved(d_mine, d_other, d, sems_d)
    for copy in copies_d:
        copy.wait()
    hidden = act.shape[0]
    delta = d[...].reshape(features, tokens)
    back = dot(down[...], delta)
    gate_pre, up_pre = pre[:hidden], pre[hidden:]
    sigmoid = 1.0 / (1.0 + jnp.exp(-gate_pre))
    d_gate = back * up_pre * sigmoid * (1.0 + gate_pre * (1.0 - sigmoid))
    d_up = back * gate_pre * sigmoid
    scale = factor[...]
    d_both = jnp.concatenate([d_gate * scale, d_up * scale], axis=0).astype(jnp.bfloat16)
    step = 8
    width = step * 2 * rows
    acts = act[...]
    copies = []

    def send_out(kind, n, src, dst):
        here = slice(n * width, (n + 1) * width)
        copy = pltpu.make_async_copy(src.at[:, here], dst.at[:, here], sems_out.at[kind, n])
        copy.start()
        copies.append(copy)

    total = jnp.zeros((1, tokens), jnp.float32)
    for n in range(chips // step):
        here = slice(n * width, (n + 1) * width)
        part = d[n * step : (n + 1) * step].reshape(width, tokens)
        grad_down[:, here] = dot(acts, part, NT).astype(jnp.bfloat16)
        send_out(0, n, grad_down, grad_down_hbm)
        floats = part.astype(jnp.float32)
        total += jnp.sum(floats * floats, axis=0, keepdims=True)
    mse[...] = jnp.sum(total, axis=1, keepdims=True) / features
    for n in range(chips // step):
        here = slice(n * width, (n + 1) * width)
        part = x[n * step : (n + 1) * step].reshape(width, tokens)
        grads = dot(d_both, part, NT)
        grad_gate[:, here] = grads[:hidden].astype(jnp.bfloat16)
        grad_up[:, here] = grads[hidden:].astype(jnp.bfloat16)
        send_out(1, n, grad_gate, grad_gate_hbm)
        send_out(2, n, grad_up, grad_up_hbm)
    for copy in copies:
        copy.wait()


def backward(d_mine, d_other, x, down, act, pre, factor):
    chips, rows, tokens = d_mine.shape
    hidden, features = down.shape
    grad = jax.ShapeDtypeStruct((hidden, features), jnp.bfloat16)
    whole = pltpu.VMEM((chips, 2, rows, tokens), jnp.bfloat16)
    return pl.pallas_call(
        backward_kernel,
        out_shape=(grad, grad, grad, jax.ShapeDtypeStruct((1, 1), jnp.float32)),
        in_specs=[anywhere()] * 2 + [vmem()] * 5,
        out_specs=(anywhere(),) * 3 + (vmem(),),
        scratch_shapes=[
            whole,
            *[pltpu.VMEM((hidden, features), jnp.bfloat16)] * 3,
            pltpu.SemaphoreType.DMA((2, PIECES)),
            pltpu.SemaphoreType.DMA((3, 8)),
        ],
        compiler_params=params(24),
        cost_estimate=cost(8),
        name="backward",
    )(d_mine, d_other, x, down, act, pre, factor)


def local(
    teacher_in,
    teacher_gain,
    routes,
    gates,
    expert_gate,
    expert_up,
    expert_down,
    projection,
    student_in,
    student_gain,
    student_gate,
    student_up,
    student_down,
):
    chips = lax.axis_size(CHIPS)
    projection_t = projection.T
    student_t = student_in.T

    arrived = exchange(dispatch(teacher_in, routes, student_t, student_gain[None, :]))
    expert_weights = (expert_gate[0], expert_up[0], expert_down[0])
    student_weights = (student_gate.T, student_up.T, student_down)
    here = student_t.shape[0]
    teacher_row = teacher_gain[None, :]
    routed = split(arrived, here, expert_weights + student_weights + (teacher_row,))
    routed_other = other_core(routed)
    first_pre, squares, cut = first_half(routed, teacher_row, *expert_weights[:2], projection_t)
    x_mine = split_student(arrived, here, routed_other, squares)
    x_other = other_core(x_mine)
    projection_other = other_core(cut)
    keep, send, token = experts(routed_other, first_pre, squares, teacher_row, *expert_weights)
    s_keep, s_send, act, pre, factor, x_all = forward(
        x_mine, x_other, routed, routed_other, *student_weights, token
    )
    outputs = merge(keep, other_core(send), projection_other)
    returned = exchange(outputs)
    joint = combine(returned, teacher_in, routes, gates, s_keep, other_core(s_send))
    near, far = targets(exchange(joint), projection_t, projection_other, student_t)
    d_mine = exchange(deltas(near, other_core(far), chips))
    d_other = other_core(d_mine)
    grad_gate, grad_up, grad_down, mse = backward(
        d_mine, d_other, x_all, student_down, act, pre, factor
    )
    return (grad_gate.T, grad_up.T, grad_down, mse.reshape(()))


def solution(mesh):
    everything = ("grp", "ep", "rep")
    placed = (
        P("ep", None),
        P(),
        P("ep", None),
        P("ep", None),
        P("ep", None, ("grp", "rep")),
        P("ep", None, ("grp", "rep")),
        P("ep", ("grp", "rep"), None),
        P(None, everything),
        P(None, everything),
        P(),
        P(None, everything),
        P(None, everything),
        P(everything, None),
    )
    return jax.shard_map(
        local,
        mesh=mesh,
        in_specs=placed,
        out_specs=(P(None, everything), P(None, everything), P(everything, None), P()),
        check_vma=False,
    )
```
